32 devices in a mesh: dom: 8 (over z, y), dir: 4 (over x, core).
Axes of the slice: x: 2, y: 2, z: 4, core: 2. Of those that a mesh axis runs over, the one named last changes fastest.
Arguments:
- action: float32 [64, 32, 4096], P('dir', None, 'dom'), may hold values from -6 to 6
- edge_angle: float32 [6, 4096], P(None, 'dom'), may hold values from -3.140625 to 3.140625
- edge_speed: float32 [6, 4096], P(None, 'dom'), may hold values from 0.3 to 3
- neighbours: int32 [6, 4096], P(None, 'dom'), may hold values from 0 to 575, as said below
- send_rows: int32 [2, 256], P(None, 'dom'), may hold values from 0 to 511, as said below
- refract_rate: float32 [32, 4096], P(None, 'dom'), may hold values from -0.45 to 0.45
- refract_angle: float32 [4096], P('dom'), may hold values from -3.140625 to 3.140625
- shift_rate: float32 [32, 4096], P(None, 'dom'), may hold values from -0.45 to 0.45
Outputs:
- wave_action: float32 [64, 32, 4096], P('dir', None, 'dom')
The draws below stay inside these ranges and needn't reach their ends.
Inputs may be any that keep to these rules, and one draw needn't show every extreme that they name: `neighbours`: slots below 512 are the partition's own nodes, then 32 slots from the lower and 32 from the upper neighbouring partition. `send_rows`: local node numbers within the sending partition.
All inputs are finite; a program needn't handle non-finite values.
Results may differ from the reference program's by a relative error of at most 0.00002.
Values sent between devices are 32-bit elements; how exact they have to be, the bound alone decides.
A program may use at most 64 MiB of HBM per device.

```python
import math
import jax
import jax.numpy as jnp
from jax import lax

NDIR = 64
NFREQ = 32
NEIGH = 6
SWEEPS = 3
NODE_DEV = 512
GHOST = 32
NODES = 4096
N_DOM = 8


def draw_neighbours(key, part):
    keys = jax.random.split(jax.random.fold_in(key, 5), 3)
    local_slots = jax.random.randint(keys[0], (NEIGH, NODES), 0, NODE_DEV, dtype=jnp.int32)
    shared_slots = jax.random.randint(keys[1], (NEIGH, NODES), NODE_DEV, NODE_DEV + 2 * GHOST, dtype=jnp.int32)
    chooser = jax.random.randint(keys[2], (NEIGH, NODES), 0, 100, dtype=jnp.int32)
    values = jnp.where(chooser < 6, shared_slots, local_slots)
    local = jnp.arange(NODES, dtype=jnp.int32) % NODE_DEV
    last_row = (jnp.arange(NEIGH, dtype=jnp.int32) == NEIGH - 1)[:, None]
    values = jnp.where(jnp.logical_and(last_row, (local == 0)[None, :]), NODE_DEV + 2 * GHOST - 1, values)
    values = jnp.where(jnp.logical_and(last_row, (local == 1)[None, :]), 0, values)
    values = jnp.where(jnp.logical_and(last_row, (local == 2)[None, :]), NODE_DEV, values)
    return values.astype(jnp.int32)


def draw_send_rows(key, part):
    parts_count = NODES // NODE_DEV
    keys = jax.random.split(jax.random.fold_in(key, 11), 2 * parts_count)

    def one_list(subkey):
        middle = jax.random.permutation(subkey, jnp.arange(1, NODE_DEV - 1, dtype=jnp.int32))[:GHOST - 2]
        picked = jnp.concatenate([jnp.array([0, NODE_DEV - 1], dtype=jnp.int32), middle])
        return jax.random.permutation(jax.random.fold_in(subkey, 7), picked)
    lists = jax.vmap(one_list)(keys)
    return lists.reshape(parts_count, 2, GHOST).transpose(1, 0, 2).reshape(2, parts_count * GHOST).astype(jnp.int32)


def steps_of(own_key, shape, pieces, low, top_value):
    def one(axis_at, shards_of):
        steps = jax.random.uniform(jax.random.fold_in(jax.random.fold_in(own_key, 6), axis_at), (shards_of,), jnp.float32, low / len(pieces), top_value / len(pieces))
        return jnp.repeat(jnp.exp(steps), shape[axis_at] // shards_of).reshape((-1,) + (1,) * (len(shape) - axis_at - 1))

    level = one(*pieces[0])
    for cut in pieces[1:]:
        level = level * one(*cut)
    return level


def bell_draw(own_key, extent, scale, bound, pieces=(), kind=jnp.bfloat16):
    gain = steps_of(own_key, extent, pieces, -0.22, 0.18) if pieces else 1.0
    result = jax.random.normal(own_key, extent, jnp.float32) * scale * gain
    return jnp.minimum(jnp.maximum(result, -bound), bound).astype(kind)


def setup_inputs(seed: int = 0) -> dict:
    splits = jax.random.split(jax.random.key(seed), 9)
    return {
        "action": bell_draw(splits[0], (NDIR, NFREQ, NODES), 1.0, 6.0, ((0, 4), (2, 8)), jnp.float32),
        "edge_angle": jnp.clip(jax.random.uniform(splits[1], (NEIGH, NODES), jnp.float32, -3.140625, 3.140625), -3.140625, 3.140625),
        "edge_speed": jnp.clip(jnp.exp(math.log(3.0) - 2.3025851 * jax.random.uniform(splits[2], (NEIGH, NODES), jnp.float32) ** steps_of(splits[2], (NEIGH, NODES), ((1, 8),), -0.2, 0.2)), 0.3, 3.0),
        "neighbours": draw_neighbours(jax.random.fold_in(splits[8], 71), 0),
        "send_rows": draw_send_rows(jax.random.fold_in(splits[8], 71), 0),
        "refract_rate": jnp.clip(jax.random.uniform(splits[5], (NFREQ, NODES), jnp.float32, -0.45, 0.45) * steps_of(splits[5], (NFREQ, NODES), ((1, 8),), -0.4, 0.0), -0.45, 0.45),
        "refract_angle": jnp.clip(jax.random.uniform(splits[6], (NODES,), jnp.float32, -3.140625, 3.140625), -3.140625, 3.140625),
        "shift_rate": jnp.clip(jax.random.uniform(splits[7], (NFREQ, NODES), jnp.float32, -0.45, 0.45) * steps_of(splits[7], (NFREQ, NODES), ((1, 8),), -0.4, 0.0), -0.45, 0.45),
    }


def reference(action, edge_angle, edge_speed, neighbours, send_rows, refract_rate, refract_angle, shift_rate):
    partition = jnp.arange(NODES, dtype=jnp.int32) // NODE_DEV
    offsets = (jnp.arange(N_DOM, dtype=jnp.int32) * NODE_DEV)[:, None]
    to_lower = send_rows[0].reshape(N_DOM, GHOST).astype(jnp.int32) + offsets
    to_upper = send_rows[1].reshape(N_DOM, GHOST).astype(jnp.int32) + offsets
    below = jnp.clip(partition - 1, 0, N_DOM - 1)[None, :]
    above = jnp.clip(partition + 1, 0, N_DOM - 1)[None, :]
    lower_index = to_upper[below, jnp.clip(neighbours - NODE_DEV, 0, GHOST - 1)]
    upper_index = to_lower[above, jnp.clip(neighbours - NODE_DEV - GHOST, 0, GHOST - 1)]
    own_index = partition[None, :] * NODE_DEV + jnp.clip(neighbours, 0, NODE_DEV - 1)
    is_own = neighbours < NODE_DEV
    is_lower = jnp.logical_and(neighbours >= NODE_DEV, neighbours < NODE_DEV + GHOST)
    source = jnp.where(is_own, own_index, jnp.where(is_lower, lower_index, upper_index)).astype(jnp.int32)
    valid = jnp.logical_or(is_own, jnp.logical_or(jnp.logical_and(is_lower, partition[None, :] > 0),
                                                  jnp.logical_and(neighbours >= NODE_DEV + GHOST, partition[None, :] < N_DOM - 1)))
    angles = (2.0 * math.pi) * jnp.arange(NDIR).astype(jnp.float32) / NDIR

    def sweep_one(inputs):
        plane, angle = inputs
        weight = edge_speed * jax.nn.relu(jnp.cos(angle - edge_angle))
        denominator = 1.0 + jnp.sum(weight, axis=0)
        field = plane
        for sweep in range(SWEEPS):
            total = plane
            for slot in range(NEIGH):
                picked = jnp.where(valid[slot][None, :], field[:, source[slot]], jnp.float32(0.0))
                total = total + weight[slot][None, :] * picked
            field = total / denominator[None, :]
        return field

    swept = lax.map(sweep_one, (action, angles))
    speed = refract_rate[None, :, :] * jnp.sin(angles[:, None, None] - refract_angle[None, None, :])
    refracted = swept - (jax.nn.relu(speed) * (swept - jnp.roll(swept, 1, 0))
                         + jnp.minimum(speed, 0.0) * (jnp.roll(swept, -1, 0) - swept))
    padded = jnp.pad(refracted, ((0, 0), (1, 1), (0, 0)))
    rate = shift_rate[None, :, :]
    return refracted - (jax.nn.relu(rate) * (refracted - padded[:, :-2, :])
                        + jnp.minimum(rate, 0.0) * (padded[:, 2:, :] - refracted))
```

```python
import functools
import math

import jax
import jax.numpy as jnp
from jax import lax
from jax.experimental import pallas as pl
from jax.experimental.pallas import tpu as pltpu
from jax.sharding import PartitionSpec as P

NDIR = 64
NEIGH = 6
SWEEPS = 3
LANES = 128
MESH = pl.DeviceIdType.MESH
UNROLL = 8


def kernel(
    sizes, action, edge_angle, edge_speed, neighbours, send_rows, refract_rate, refract_angle, shift_rate,
    out, f0, f1, f2, f3, scaled, weights, columns, swept, bearing, sends, halo,
    send_sem, recv_sem, dir_send, dir_recv,
):
    sector, freqs, nodes, ghost, groups, n_dom, n_dir = sizes
    fields = (f0, f1, f2, f3)
    dom = lax.axis_index("dom")
    here = lax.axis_index("dir")
    has_lower = dom > 0
    has_upper = dom < n_dom - 1
    next_dir = lax.rem(here + 1, n_dir)
    prev_dir = lax.rem(here + n_dir - 1, n_dir)

    barrier = pltpu.get_barrier_semaphore()
    for other in (next_dir, prev_dir):
        pl.semaphore_signal(barrier, inc=1, device_id=(dom, other), device_id_type=MESH)

    @pl.when(has_lower)
    def _():
        pl.semaphore_signal(barrier, inc=1, device_id=(dom - 1, here), device_id_type=MESH)

    @pl.when(has_upper)
    def _():
        pl.semaphore_signal(barrier, inc=1, device_id=(dom + 1, here), device_id_type=MESH)

    low_at, high_at, width = nodes * groups, (nodes + ghost) * groups, ghost * groups

    @pl.when(dom == 0)
    def _():
        for field in (f0, f1, f2):
            field[pl.ds(low_at, width), :] = jnp.zeros((width, LANES), jnp.float32)

    @pl.when(dom == n_dom - 1)
    def _():
        for field in (f0, f1, f2):
            field[pl.ds(high_at, width), :] = jnp.zeros((width, LANES), jnp.float32)

    def to_lower(sweep):
        return pltpu.make_async_remote_copy(
            src_ref=sends.at[sweep, 0], dst_ref=fields[sweep].at[pl.ds(high_at, width)],
            send_sem=send_sem.at[sweep, 0], recv_sem=recv_sem.at[sweep, 0],
            device_id=(dom - 1, here), device_id_type=MESH)

    def to_upper(sweep):
        return pltpu.make_async_remote_copy(
            src_ref=sends.at[sweep, 1], dst_ref=fields[sweep].at[pl.ds(low_at, width)],
            send_sem=send_sem.at[sweep, 1], recv_sem=recv_sem.at[sweep, 1],
            device_id=(dom + 1, here), device_id_type=MESH)

    def start(sweep):
        @pl.when(has_lower)
        def _():
            to_lower(sweep).start()

        @pl.when(has_upper)
        def _():
            to_upper(sweep).start()

    def arrived(sweep):
        @pl.when(has_lower)
        def _():
            to_upper(sweep).wait_recv()

        @pl.when(has_upper)
        def _():
            to_lower(sweep).wait_recv()

    for tile in range(nodes // LANES):
        for group in range(groups):
            block = action[:, group * 8:(group + 1) * 8, tile * LANES:(tile + 1) * LANES]
            turned = block.reshape(LANES, LANES).T
            f0[pl.ds(tile * LANES * groups + group, LANES, stride=groups), :] = turned
            scaled[pl.ds(tile * LANES * groups + group, LANES, stride=groups), :] = turned

    @pl.loop(0, ghost // UNROLL)
    def _(step):
        for u in range(UNROLL):
            at = step * UNROLL + u
            for side in range(2):
                node = send_rows[side, at]
                sends[0, side, pl.ds(at * groups, groups), :] = scaled[pl.ds(node * groups, groups), :]

    pl.semaphore_wait(barrier, 2 + has_lower.astype(jnp.int32) + has_upper.astype(jnp.int32))
    start(0)

    first_dir = here * sector
    turn = 2.0 * math.pi / NDIR
    lane_dir = first_dir + lax.broadcasted_iota(jnp.int32, (8, LANES), 1) // 8
    lane_angle = lane_dir.astype(jnp.float32) * turn
    lane_cos, lane_sin = jnp.cos(lane_angle)[:1], jnp.sin(lane_angle)[:1]
    row_dir = first_dir + lax.broadcasted_iota(jnp.int32, (sector, nodes), 0)
    turned = jnp.sin(row_dir.astype(jnp.float32) * turn - refract_angle[...])
    for d in range(sector):
        bearing[d] = turned[d:d + 1]
    gap = jnp.zeros((8 - NEIGH, nodes), jnp.float32)
    edge_cos = edge_speed[...] * jnp.cos(edge_angle[...])
    edge_sin = edge_speed[...] * jnp.sin(edge_angle[...])
    parts = jnp.concatenate([edge_cos, gap, edge_sin, gap], axis=0)
    columns[...] = parts.T

    rows = 32

    @pl.loop(0, nodes // rows)
    def _(step):
        at = pl.multiple_of(step * rows, rows)
        block = columns[pl.ds(at, rows), :]
        found = []
        total = jnp.ones((rows, LANES), jnp.float32)
        for slot in range(NEIGH):
            weight = jnp.maximum(block[:, slot:slot + 1] * lane_cos + block[:, 8 + slot:9 + slot] * lane_sin, 0.0)
            found.append(weight)
            total = total + weight
        inverse = 1.0 / total
        for slot in range(NEIGH):
            weights[pl.ds(slot * nodes + at, rows), :] = found[slot] * inverse
        for group in range(groups):
            where = pl.ds(at * groups + group, rows, stride=groups)
            scaled[where, :] = scaled[where, :] * inverse

    def update(field, node):
        total = scaled[pl.ds(node * groups, groups), :]
        for slot in range(NEIGH):
            picked = field[pl.ds(neighbours[slot, node] * groups, groups), :]
            total = total + weights[pl.ds(slot * nodes + node, 1), :] * picked
        return total

    for sweep in range(SWEEPS):
        field, result = fields[sweep], fields[sweep + 1]
        arrived(sweep)
        if sweep < SWEEPS - 1:
            @pl.loop(0, ghost // 4)
            def _(step):
                for u in range(4):
                    at = step * 4 + u
                    for side in range(2):
                        sends[sweep + 1, side, pl.ds(at * groups, groups), :] = update(field, send_rows[side, at])

            start(sweep + 1)

        @pl.loop(0, nodes // UNROLL)
        def _(step):
            for u in range(UNROLL):
                node = step * UNROLL + u
                result[pl.ds(node * groups, groups), :] = update(field, node)

    for tile in range(nodes // LANES):
        for group in range(groups):
            block = f3[pl.ds(tile * LANES * groups + group, LANES, stride=groups), :].T
            swept[:, group * 8:(group + 1) * 8, tile * LANES:(tile + 1) * LANES] = block.reshape(sector, 8, LANES)

    up = pltpu.make_async_remote_copy(
        src_ref=swept.at[sector - 1], dst_ref=halo.at[0], send_sem=dir_send.at[0], recv_sem=dir_recv.at[0],
        device_id=(dom, next_dir), device_id_type=MESH)
    down = pltpu.make_async_remote_copy(
        src_ref=swept.at[0], dst_ref=halo.at[1], send_sem=dir_send.at[1], recv_sem=dir_recv.at[1],
        device_id=(dom, prev_dir), device_id_type=MESH)
    up.start()
    down.start()

    freq = lax.broadcasted_iota(jnp.int32, (freqs, LANES), 0)

    def finish(d, before, after):
        for tile in range(nodes // LANES):
            at = pl.ds(tile * LANES, LANES)
            own = swept[d, :, at]
            speed = refract_rate[:, at] * bearing[d, :, at]
            refracted = own - (jnp.maximum(speed, 0.0) * (own - before(at)) + jnp.minimum(speed, 0.0) * (after(at) - own))
            lower = jnp.where(freq == 0, 0.0, pltpu.roll(refracted, 1, 0))
            upper = jnp.where(freq == freqs - 1, 0.0, pltpu.roll(refracted, freqs - 1, 0))
            rate = shift_rate[:, at]
            out[d, :, at] = refracted - (
                jnp.maximum(rate, 0.0) * (refracted - lower) + jnp.minimum(rate, 0.0) * (upper - refracted))

    @pl.loop(1, sector - 1)
    def _(d):
        finish(d, lambda at: swept[d - 1, :, at], lambda at: swept[d + 1, :, at])

    up.wait()
    finish(0, lambda at: halo[0, :, at], lambda at: swept[1, :, at])
    down.wait()
    finish(sector - 1, lambda at: swept[sector - 2, :, at], lambda at: halo[1, :, at])

    for sweep in range(SWEEPS):
        @pl.when(has_lower)
        def _():
            to_lower(sweep).wait_send()

        @pl.when(has_upper)
        def _():
            to_upper(sweep).wait_send()


def shards(
    action, edge_angle, edge_speed, neighbours, send_rows, refract_rate, refract_angle, shift_rate
):
    sector, freqs, nodes = action.shape
    ghost = send_rows.shape[1]
    groups = freqs // 8
    sizes = (sector, freqs, nodes, ghost, groups, lax.axis_size("dom"), lax.axis_size("dir"))
    vmem = pl.BlockSpec(memory_space=pltpu.VMEM)
    smem = pl.BlockSpec(memory_space=pltpu.SMEM)
    field = pltpu.VMEM(((nodes + 2 * ghost) * groups, LANES), jnp.float32)
    local = pltpu.VMEM((nodes * groups, LANES), jnp.float32)
    return pl.pallas_call(
        functools.partial(kernel, sizes),
        out_shape=jax.ShapeDtypeStruct(action.shape, jnp.float32),
        in_specs=[vmem, vmem, vmem, smem, smem, vmem, vmem, vmem],
        out_specs=vmem,
        scratch_shapes=[
            field, field, field, local, local,
            pltpu.VMEM((NEIGH * nodes, LANES), jnp.float32),
            pltpu.VMEM((nodes, 16), jnp.float32),
            pltpu.VMEM((sector, freqs, nodes), jnp.float32),
            pltpu.VMEM((sector, 1, nodes), jnp.float32),
            pltpu.VMEM((SWEEPS, 2, ghost * groups, LANES), jnp.float32),
            pltpu.VMEM((2, freqs, nodes), jnp.float32),
            pltpu.SemaphoreType.DMA((SWEEPS, 2)),
            pltpu.SemaphoreType.DMA((SWEEPS, 2)),
            pltpu.SemaphoreType.DMA((2,)),
            pltpu.SemaphoreType.DMA((2,)),
        ],
        compiler_params=pltpu.CompilerParams(
            collective_id=0, has_side_effects=True, vmem_limit_bytes=32 * 1024 * 1024),
    )(action, edge_angle, edge_speed, neighbours, send_rows, refract_rate,
      refract_angle.reshape(1, nodes), shift_rate)


def solution(mesh):
    return jax.shard_map(
        shards,
        mesh=mesh,
        in_specs=(
            P("dir", None, "dom"),
            P(None, "dom"),
            P(None, "dom"),
            P(None, "dom"),
            P(None, "dom"),
            P(None, "dom"),
            P("dom"),
            P(None, "dom"),
        ),
        out_specs=P("dir", None, "dom"),
        check_vma=False,
    )
```

```python
import functools
import math

import jax
import jax.numpy as jnp
from jax import lax
from jax.experimental import pallas as pl
from jax.experimental.pallas import tpu as pltpu
from jax.sharding import PartitionSpec as P

NDIR = 64
NEIGH = 6
SWEEPS = 3
LANES = 128
MESH = pl.DeviceIdType.MESH
UNROLL = 8
BATCH = 32


def kernel(
    sizes, action_hbm, edge_angle_hbm, edge_speed_hbm, neighbours_hbm, send_rows_hbm, refract_rate_hbm,
    refract_angle_hbm, shift_rate_hbm, out_hbm,
    action, edge_angle, edge_speed, neighbours, send_rows, refract_rate, refract_angle, shift_rate,
    shared, slots, table, in_sem, out, out_sem, f0, f1, f2, f3, scaled, weights, columns, swept, bearing, sends, halo,
    send_sem, recv_sem, dir_send, dir_recv,
):
    sector, freqs, nodes, ghost, groups, n_dom, n_dir = sizes
    fields = (f0, f1, f2, f3)
    dom = lax.axis_index("dom")
    here = lax.axis_index("dir")
    has_lower = dom > 0
    has_upper = dom < n_dom - 1
    next_dir = lax.rem(here + 1, n_dir)
    prev_dir = lax.rem(here + n_dir - 1, n_dir)

    loads = [
        pltpu.make_async_copy(source, target, in_sem.at[at]) for at, (source, target) in enumerate((
            (send_rows_hbm, send_rows), (neighbours_hbm, neighbours), (edge_angle_hbm, edge_angle),
            (edge_speed_hbm, edge_speed), (refract_angle_hbm, refract_angle),
            (refract_rate_hbm, refract_rate), (shift_rate_hbm, shift_rate), (neighbours_hbm, shared)))]
    planes = [
        pltpu.make_async_copy(
            action_hbm.at[:, pl.ds(group * 8, 8), :], action.at[:, pl.ds(group * 8, 8), :], in_sem.at[9 + group])
        for group in range(groups)]
    for load in loads[:2] + planes + loads[2:]:
        load.start()

    barrier = pltpu.get_barrier_semaphore()
    for other in (next_dir, prev_dir):
        pl.semaphore_signal(barrier, inc=1, device_id=(dom, other), device_id_type=MESH)

    @pl.when(has_lower)
    def _():
        pl.semaphore_signal(barrier, inc=1, device_id=(dom - 1, here), device_id_type=MESH)

    @pl.when(has_upper)
    def _():
        pl.semaphore_signal(barrier, inc=1, device_id=(dom + 1, here), device_id_type=MESH)

    low_at, high_at, width = nodes * groups, (nodes + ghost) * groups, ghost * groups

    @pl.when(dom == 0)
    def _():
        for field in (f0, f1, f2):
            field[pl.ds(low_at, width), :] = jnp.zeros((width, LANES), jnp.float32)

    @pl.when(dom == n_dom - 1)
    def _():
        for field in (f0, f1, f2):
            field[pl.ds(high_at, width), :] = jnp.zeros((width, LANES), jnp.float32)

    def to_lower(sweep):
        return pltpu.make_async_remote_copy(
            src_ref=sends.at[sweep, 0], dst_ref=fields[sweep].at[pl.ds(high_at, width)],
            send_sem=send_sem.at[sweep, 0], recv_sem=recv_sem.at[sweep, 0],
            device_id=(dom - 1, here), device_id_type=MESH)

    def to_upper(sweep):
        return pltpu.make_async_remote_copy(
            src_ref=sends.at[sweep, 1], dst_ref=fields[sweep].at[pl.ds(low_at, width)],
            send_sem=send_sem.at[sweep, 1], recv_sem=recv_sem.at[sweep, 1],
            device_id=(dom + 1, here), device_id_type=MESH)

    def start(sweep):
        @pl.when(has_lower)
        def _():
            to_lower(sweep).start()

        @pl.when(has_upper)
        def _():
            to_upper(sweep).start()

    def arrived(sweep):
        @pl.when(has_lower)
        def _():
            to_upper(sweep).wait_recv()

        @pl.when(has_upper)
        def _():
            to_lower(sweep).wait_recv()

    loads[1].wait()
    slots[...] = jnp.zeros_like(slots)
    for tile in range(nodes // LANES):
        slots[tile * 8:tile * 8 + NEIGH, :] = neighbours[:, tile * LANES:(tile + 1) * LANES] * groups
    to_table = pltpu.make_async_copy(slots, table, in_sem.at[8])
    to_table.start()
    for group in range(groups):
        planes[group].wait()
        for tile in range(nodes // LANES):
            block = action[:, group * 8:(group + 1) * 8, tile * LANES:(tile + 1) * LANES]
            turned = block.reshape(LANES, LANES).T
            f0[pl.ds(tile * LANES * groups + group, LANES, stride=groups), :] = turned
            scaled[pl.ds(tile * LANES * groups + group, LANES, stride=groups), :] = turned

    loads[0].wait()

    @pl.loop(0, ghost // UNROLL)
    def _(step):
        for u in range(UNROLL):
            at = step * UNROLL + u
            for side in range(2):
                node = send_rows[side, at]
                sends[0, side, pl.ds(at * groups, groups), :] = scaled[pl.ds(node * groups, groups), :]

    pl.semaphore_wait(barrier, 2 + has_lower.astype(jnp.int32) + has_upper.astype(jnp.int32))
    start(0)

    for load in loads[2:]:
        load.wait()
    first_dir = here * sector
    turn = 2.0 * math.pi / NDIR
    lane_dir = first_dir + lax.broadcasted_iota(jnp.int32, (8, LANES), 1) // 8
    lane_angle = lane_dir.astype(jnp.float32) * turn
    lane_cos, lane_sin = jnp.cos(lane_angle)[:1], jnp.sin(lane_angle)[:1]
    row_dir = first_dir + lax.broadcasted_iota(jnp.int32, (sector, nodes), 0)
    turned = jnp.sin(row_dir.astype(jnp.float32) * turn - refract_angle[...])
    for d in range(sector):
        bearing[d] = turned[d:d + 1]
    gap = jnp.zeros((8 - NEIGH, nodes), jnp.float32)
    edge_cos = edge_speed[...] * jnp.cos(edge_angle[...])
    edge_sin = edge_speed[...] * jnp.sin(edge_angle[...])
    parts = jnp.concatenate([edge_cos, gap, edge_sin, gap], axis=0)
    columns[...] = parts.T

    rows = 32

    @pl.loop(0, nodes // rows)
    def _(step):
        at = pl.multiple_of(step * rows, rows)
        block = columns[pl.ds(at, rows), :]
        found = []
        total = jnp.ones((rows, LANES), jnp.float32)
        for slot in range(NEIGH):
            weight = jnp.maximum(block[:, slot:slot + 1] * lane_cos + block[:, 8 + slot:9 + slot] * lane_sin, 0.0)
            found.append(weight)
            total = total + weight
        inverse = 1.0 / total
        for slot in range(NEIGH):
            weights[pl.ds(slot * nodes + at, rows), :] = found[slot] * inverse
        for group in range(groups):
            where = pl.ds(at * groups + group, rows, stride=groups)
            scaled[where, :] = scaled[where, :] * inverse

    to_table.wait()

    def update(field, node, row_of):
        total = scaled[pl.ds(node * groups, groups), :]
        for slot in range(NEIGH):
            picked = field[pl.ds(row_of(slot), groups), :]
            total = total + weights[pl.ds(slot * nodes + node, 1), :] * picked
        return total

    for sweep in range(SWEEPS):
        field, result = fields[sweep], fields[sweep + 1]
        arrived(sweep)
        if sweep < SWEEPS - 1:
            @pl.loop(0, ghost // 4)
            def _(step):
                for u in range(4):
                    at = step * 4 + u
                    for side in range(2):
                        node = send_rows[side, at]
                        sends[sweep + 1, side, pl.ds(at * groups, groups), :] = update(
                            field, node, lambda slot: shared[slot, node] * groups)

            start(sweep + 1)

        @pl.loop(0, nodes // LANES)
        def _(tile):
            @pl.loop(0, LANES // BATCH)
            def _(step):
                for u in range(BATCH):
                    lane = step * BATCH + u
                    node = tile * LANES + lane
                    result[pl.ds(node * groups, groups), :] = update(
                        field, node, lambda slot: table[tile * 8 + slot, lane])

    for tile in range(nodes // LANES):
        for group in range(groups):
            block = f3[pl.ds(tile * LANES * groups + group, LANES, stride=groups), :].T
            swept[:, group * 8:(group + 1) * 8, tile * LANES:(tile + 1) * LANES] = block.reshape(sector, 8, LANES)

    up = pltpu.make_async_remote_copy(
        src_ref=swept.at[sector - 1], dst_ref=halo.at[0], send_sem=dir_send.at[0], recv_sem=dir_recv.at[0],
        device_id=(dom, next_dir), device_id_type=MESH)
    down = pltpu.make_async_remote_copy(
        src_ref=swept.at[0], dst_ref=halo.at[1], send_sem=dir_send.at[1], recv_sem=dir_recv.at[1],
        device_id=(dom, prev_dir), device_id_type=MESH)
    up.start()
    down.start()

    freq = lax.broadcasted_iota(jnp.int32, (freqs, LANES), 0)

    def stored(d):
        return pltpu.make_async_copy(out.at[d], out_hbm.at[d], out_sem.at[d])

    def finish(d, before, after):
        for tile in range(nodes // LANES):
            at = pl.ds(tile * LANES, LANES)
            own = swept[d, :, at]
            speed = refract_rate[:, at] * bearing[d, :, at]
            refracted = own - (jnp.maximum(speed, 0.0) * (own - before(at)) + jnp.minimum(speed, 0.0) * (after(at) - own))
            lower = jnp.where(freq == 0, 0.0, pltpu.roll(refracted, 1, 0))
            upper = jnp.where(freq == freqs - 1, 0.0, pltpu.roll(refracted, freqs - 1, 0))
            rate = shift_rate[:, at]
            out[d, :, at] = refracted - (
                jnp.maximum(rate, 0.0) * (refracted - lower) + jnp.minimum(rate, 0.0) * (upper - refracted))

        stored(d).start()

    @pl.loop(1, sector - 1)
    def _(d):
        finish(d, lambda at: swept[d - 1, :, at], lambda at: swept[d + 1, :, at])

    up.wait()
    finish(0, lambda at: halo[0, :, at], lambda at: swept[1, :, at])
    down.wait()
    finish(sector - 1, lambda at: swept[sector - 2, :, at], lambda at: halo[1, :, at])

    for sweep in range(SWEEPS):
        @pl.when(has_lower)
        def _():
            to_lower(sweep).wait_send()

        @pl.when(has_upper)
        def _():
            to_upper(sweep).wait_send()

    @pl.loop(0, sector)
    def _(d):
        stored(d).wait()


def shards(
    action, edge_angle, edge_speed, neighbours, send_rows, refract_rate, refract_angle, shift_rate
):
    sector, freqs, nodes = action.shape
    ghost = send_rows.shape[1]
    groups = freqs // 8
    sizes = (sector, freqs, nodes, ghost, groups, lax.axis_size("dom"), lax.axis_size("dir"))
    field = pltpu.VMEM(((nodes + 2 * ghost) * groups, LANES), jnp.float32)
    local = pltpu.VMEM((nodes * groups, LANES), jnp.float32)
    return pl.pallas_call(
        functools.partial(kernel, sizes),
        out_shape=jax.ShapeDtypeStruct(action.shape, jnp.float32),
        in_specs=[pl.BlockSpec(memory_space=pltpu.HBM)] * 8,
        out_specs=pl.BlockSpec(memory_space=pltpu.HBM),
        scratch_shapes=[
            pltpu.VMEM(action.shape, jnp.float32),
            pltpu.VMEM(edge_angle.shape, jnp.float32),
            pltpu.VMEM(edge_speed.shape, jnp.float32),
            pltpu.VMEM(neighbours.shape, jnp.int32),
            pltpu.SMEM(send_rows.shape, jnp.int32),
            pltpu.VMEM(refract_rate.shape, jnp.float32),
            pltpu.VMEM((1, nodes), jnp.float32),
            pltpu.VMEM(shift_rate.shape, jnp.float32),
            pltpu.SMEM(neighbours.shape, jnp.int32),
            pltpu.VMEM((nodes // LANES * 8, LANES), jnp.int32),
            pltpu.SMEM((nodes // LANES * 8, LANES), jnp.int32),
            pltpu.SemaphoreType.DMA((9 + groups,)),
            pltpu.VMEM(action.shape, jnp.float32),
            pltpu.SemaphoreType.DMA((sector,)),
            field, field, field, local, local,
            pltpu.VMEM((NEIGH * nodes, LANES), jnp.float32),
            pltpu.VMEM((nodes, 16), jnp.float32),
            pltpu.VMEM((sector, freqs, nodes), jnp.float32),
            pltpu.VMEM((sector, 1, nodes), jnp.float32),
            pltpu.VMEM((SWEEPS, 2, ghost * groups, LANES), jnp.float32),
            pltpu.VMEM((2, freqs, nodes), jnp.float32),
            pltpu.SemaphoreType.DMA((SWEEPS, 2)),
            pltpu.SemaphoreType.DMA((SWEEPS, 2)),
            pltpu.SemaphoreType.DMA((2,)),
            pltpu.SemaphoreType.DMA((2,)),
        ],
        compiler_params=pltpu.CompilerParams(
            collective_id=0, has_side_effects=True, vmem_limit_bytes=64 * 1024 * 1024),
    )(action, edge_angle, edge_speed, neighbours, send_rows, refract_rate,
      refract_angle.reshape(1, nodes), shift_rate)


def solution(mesh):
    return jax.shard_map(
        shards,
        mesh=mesh,
        in_specs=(
            P("dir", None, "dom"),
            P(None, "dom"),
            P(None, "dom"),
            P(None, "dom"),
            P(None, "dom"),
            P(None, "dom"),
            P("dom"),
            P(None, "dom"),
        ),
        out_specs=P("dir", None, "dom"),
        check_vma=False,
    )
```

```python
import functools
import math

import jax
import jax.numpy as jnp
from jax import lax
from jax.experimental import pallas as pl
from jax.experimental.pallas import tpu as pltpu
from jax.sharding import PartitionSpec as P

NDIR = 64
NEIGH = 6
SWEEPS = 3
LANES = 128
MESH = pl.DeviceIdType.MESH
UNROLL = 8
BATCH = 32


def kernel(
    sizes, action_hbm, edge_angle_hbm, edge_speed_hbm, neighbours_hbm, send_rows_hbm, refract_rate_hbm,
    refract_angle_hbm, shift_rate_hbm, out,
    action, edge_angle, edge_speed, neighbours, send_rows, refract_rate, refract_angle, shift_rate,
    shared, slots, table, in_sem, f0, f1, f2, f3, scaled, weights, columns, swept, bearing, sends, halo,
    send_sem, recv_sem, dir_send, dir_recv,
):
    sector, freqs, nodes, ghost, groups, n_dom, n_dir = sizes
    fields = (f0, f1, f2, f3)
    dom = lax.axis_index("dom")
    here = lax.axis_index("dir")
    has_lower = dom > 0
    has_upper = dom < n_dom - 1
    next_dir = lax.rem(here + 1, n_dir)
    prev_dir = lax.rem(here + n_dir - 1, n_dir)

    loads = [
        pltpu.make_async_copy(source, target, in_sem.at[at]) for at, (source, target) in enumerate((
            (send_rows_hbm, send_rows), (neighbours_hbm, neighbours), (edge_angle_hbm, edge_angle),
            (edge_speed_hbm, edge_speed), (refract_angle_hbm, refract_angle),
            (refract_rate_hbm, refract_rate), (shift_rate_hbm, shift_rate), (neighbours_hbm, shared)))]
    planes = [
        pltpu.make_async_copy(
            action_hbm.at[:, pl.ds(group * 8, 8), :], action.at[:, pl.ds(group * 8, 8), :], in_sem.at[9 + group])
        for group in range(groups)]
    for load in loads[:2] + planes + loads[2:]:
        load.start()

    barrier = pltpu.get_barrier_semaphore()
    for other in (next_dir, prev_dir):
        pl.semaphore_signal(barrier, inc=1, device_id=(dom, other), device_id_type=MESH)

    @pl.when(has_lower)
    def _():
        pl.semaphore_signal(barrier, inc=1, device_id=(dom - 1, here), device_id_type=MESH)

    @pl.when(has_upper)
    def _():
        pl.semaphore_signal(barrier, inc=1, device_id=(dom + 1, here), device_id_type=MESH)

    low_at, high_at, width = nodes * groups, (nodes + ghost) * groups, ghost * groups

    @pl.when(dom == 0)
    def _():
        for field in (f0, f1, f2):
            field[pl.ds(low_at, width), :] = jnp.zeros((width, LANES), jnp.float32)

    @pl.when(dom == n_dom - 1)
    def _():
        for field in (f0, f1, f2):
            field[pl.ds(high_at, width), :] = jnp.zeros((width, LANES), jnp.float32)

    def to_lower(sweep):
        return pltpu.make_async_remote_copy(
            src_ref=sends.at[sweep, 0], dst_ref=fields[sweep].at[pl.ds(high_at, width)],
            send_sem=send_sem.at[sweep, 0], recv_sem=recv_sem.at[sweep, 0],
            device_id=(dom - 1, here), device_id_type=MESH)

    def to_upper(sweep):
        return pltpu.make_async_remote_copy(
            src_ref=sends.at[sweep, 1], dst_ref=fields[sweep].at[pl.ds(low_at, width)],
            send_sem=send_sem.at[sweep, 1], recv_sem=recv_sem.at[sweep, 1],
            device_id=(dom + 1, here), device_id_type=MESH)

    def start(sweep):
        @pl.when(has_lower)
        def _():
            to_lower(sweep).start()

        @pl.when(has_upper)
        def _():
            to_upper(sweep).start()

    def arrived(sweep):
        @pl.when(has_lower)
        def _():
            to_upper(sweep).wait_recv()

        @pl.when(has_upper)
        def _():
            to_lower(sweep).wait_recv()

    loads[1].wait()
    slots[...] = jnp.zeros_like(slots)
    for tile in range(nodes // LANES):
        slots[tile * 8:tile * 8 + NEIGH, :] = neighbours[:, tile * LANES:(tile + 1) * LANES] * groups
    to_table = pltpu.make_async_copy(slots, table, in_sem.at[8])
    to_table.start()
    for group in range(groups):
        planes[group].wait()
        for tile in range(nodes // LANES):
            block = action[:, group * 8:(group + 1) * 8, tile * LANES:(tile + 1) * LANES]
            turned = block.reshape(LANES, LANES).T
            f0[pl.ds(tile * LANES * groups + group, LANES, stride=groups), :] = turned
            scaled[pl.ds(tile * LANES * groups + group, LANES, stride=groups), :] = turned

    loads[0].wait()

    @pl.loop(0, ghost // UNROLL)
    def _(step):
        picked = [
            scaled[pl.ds(send_rows[side, step * UNROLL + u] * groups, groups), :]
            for u in range(UNROLL) for side in range(2)]
        for u in range(UNROLL):
            for side in range(2):
                sends[0, side, pl.ds((step * UNROLL + u) * groups, groups), :] = picked[2 * u + side]

    pl.semaphore_wait(barrier, 2 + has_lower.astype(jnp.int32) + has_upper.astype(jnp.int32))
    start(0)

    for load in loads[2:]:
        load.wait()
    first_dir = here * sector
    turn = 2.0 * math.pi / NDIR
    lane_dir = first_dir + lax.broadcasted_iota(jnp.int32, (8, LANES), 1) // 8
    lane_angle = lane_dir.astype(jnp.float32) * turn
    lane_cos, lane_sin = jnp.cos(lane_angle)[:1], jnp.sin(lane_angle)[:1]
    row_dir = first_dir + lax.broadcasted_iota(jnp.int32, (sector, nodes), 0)
    turned = jnp.sin(row_dir.astype(jnp.float32) * turn - refract_angle[...])
    for d in range(sector):
        bearing[d] = turned[d:d + 1]
    gap = jnp.zeros((8 - NEIGH, nodes), jnp.float32)
    edge_cos = edge_speed[...] * jnp.cos(edge_angle[...])
    edge_sin = edge_speed[...] * jnp.sin(edge_angle[...])
    parts = jnp.concatenate([edge_cos, gap, edge_sin, gap], axis=0)
    columns[...] = parts.T

    rows = 32

    @pl.loop(0, nodes // rows)
    def _(step):
        at = pl.multiple_of(step * rows, rows)
        block = columns[pl.ds(at, rows), :]
        places = [pl.ds(at * groups + group, rows, stride=groups) for group in range(groups)]
        base = [scaled[place, :] for place in places]
        found = []
        total = jnp.ones((rows, LANES), jnp.float32)
        for slot in range(NEIGH):
            weight = jnp.maximum(block[:, slot:slot + 1] * lane_cos + block[:, 8 + slot:9 + slot] * lane_sin, 0.0)
            found.append(weight)
            total = total + weight
        inverse = 1.0 / total
        for slot in range(NEIGH):
            weights[pl.ds(slot * nodes + at, rows), :] = found[slot] * inverse
        for group in range(groups):
            scaled[places[group], :] = base[group] * inverse

    to_table.wait()

    def update(field, node, row_of):
        total = scaled[pl.ds(node * groups, groups), :]
        for slot in range(NEIGH):
            picked = field[pl.ds(row_of(slot), groups), :]
            total = total + weights[pl.ds(slot * nodes + node, 1), :] * picked
        return total

    for sweep in range(SWEEPS):
        field, result = fields[sweep], fields[sweep + 1]
        arrived(sweep)
        if sweep < SWEEPS - 1:
            @pl.loop(0, ghost // UNROLL)
            def _(step):
                totals = []
                for u in range(UNROLL):
                    for side in range(2):
                        node = send_rows[side, step * UNROLL + u]
                        totals.append(update(field, node, lambda slot, node=node: shared[slot, node] * groups))
                for u in range(UNROLL):
                    for side in range(2):
                        sends[sweep + 1, side, pl.ds((step * UNROLL + u) * groups, groups), :] = totals[2 * u + side]

            start(sweep + 1)

        @pl.loop(0, nodes // LANES)
        def _(tile):
            @pl.loop(0, LANES // BATCH)
            def _(step):
                totals = []
                for u in range(BATCH):
                    lane = step * BATCH + u
                    totals.append(update(
                        field, tile * LANES + lane, lambda slot, lane=lane: table[tile * 8 + slot, lane]))
                for u in range(BATCH):
                    node = tile * LANES + step * BATCH + u
                    result[pl.ds(node * groups, groups), :] = totals[u]

    for tile in range(nodes // LANES):
        for group in range(groups):
            block = f3[pl.ds(tile * LANES * groups + group, LANES, stride=groups), :].T
            swept[:, group * 8:(group + 1) * 8, tile * LANES:(tile + 1) * LANES] = block.reshape(sector, 8, LANES)

    up = pltpu.make_async_remote_copy(
        src_ref=swept.at[sector - 1], dst_ref=halo.at[0], send_sem=dir_send.at[0], recv_sem=dir_recv.at[0],
        device_id=(dom, next_dir), device_id_type=MESH)
    down = pltpu.make_async_remote_copy(
        src_ref=swept.at[0], dst_ref=halo.at[1], send_sem=dir_send.at[1], recv_sem=dir_recv.at[1],
        device_id=(dom, prev_dir), device_id_type=MESH)
    up.start()
    down.start()

    freq = lax.broadcasted_iota(jnp.int32, (freqs, LANES), 0)

    def finish(d, before, after):
        places = [pl.ds(tile * LANES, LANES) for tile in range(nodes // LANES)]
        found = []
        for at in places:
            own = swept[d, :, at]
            speed = refract_rate[:, at] * bearing[d, :, at]
            refracted = own - (jnp.maximum(speed, 0.0) * (own - before(at)) + jnp.minimum(speed, 0.0) * (after(at) - own))
            lower = jnp.where(freq == 0, 0.0, pltpu.roll(refracted, 1, 0))
            upper = jnp.where(freq == freqs - 1, 0.0, pltpu.roll(refracted, freqs - 1, 0))
            rate = shift_rate[:, at]
            found.append(refracted - (
                jnp.maximum(rate, 0.0) * (refracted - lower) + jnp.minimum(rate, 0.0) * (upper - refracted)))
        for at, value in zip(places, found):
            out[d, :, at] = value

    @pl.loop(1, sector - 1)
    def _(d):
        finish(d, lambda at: swept[d - 1, :, at], lambda at: swept[d + 1, :, at])

    up.wait()
    finish(0, lambda at: halo[0, :, at], lambda at: swept[1, :, at])
    down.wait()
    finish(sector - 1, lambda at: swept[sector - 2, :, at], lambda at: halo[1, :, at])

    for sweep in range(SWEEPS):
        @pl.when(has_lower)
        def _():
            to_lower(sweep).wait_send()

        @pl.when(has_upper)
        def _():
            to_upper(sweep).wait_send()


def shards(
    action, edge_angle, edge_speed, neighbours, send_rows, refract_rate, refract_angle, shift_rate
):
    sector, freqs, nodes = action.shape
    ghost = send_rows.shape[1]
    groups = freqs // 8
    sizes = (sector, freqs, nodes, ghost, groups, lax.axis_size("dom"), lax.axis_size("dir"))
    field = pltpu.VMEM(((nodes + 2 * ghost) * groups, LANES), jnp.float32)
    local = pltpu.VMEM((nodes * groups, LANES), jnp.float32)
    return pl.pallas_call(
        functools.partial(kernel, sizes),
        out_shape=pltpu.VMEM(action.shape, jnp.float32),
        in_specs=[pl.BlockSpec(memory_space=pltpu.HBM)] * 8,
        out_specs=pl.BlockSpec(memory_space=pltpu.VMEM),
        scratch_shapes=[
            pltpu.VMEM(action.shape, jnp.float32),
            pltpu.VMEM(edge_angle.shape, jnp.float32),
            pltpu.VMEM(edge_speed.shape, jnp.float32),
            pltpu.VMEM(neighbours.shape, jnp.int32),
            pltpu.SMEM(send_rows.shape, jnp.int32),
            pltpu.VMEM(refract_rate.shape, jnp.float32),
            pltpu.VMEM((1, nodes), jnp.float32),
            pltpu.VMEM(shift_rate.shape, jnp.float32),
            pltpu.SMEM(neighbours.shape, jnp.int32),
            pltpu.VMEM((nodes // LANES * 8, LANES), jnp.int32),
            pltpu.SMEM((nodes // LANES * 8, LANES), jnp.int32),
            pltpu.SemaphoreType.DMA((9 + groups,)),
            field, field, field, local, local,
            pltpu.VMEM((NEIGH * nodes, LANES), jnp.float32),
            pltpu.VMEM((nodes, 16), jnp.float32),
            pltpu.VMEM((sector, freqs, nodes), jnp.float32),
            pltpu.VMEM((sector, 1, nodes), jnp.float32),
            pltpu.VMEM((SWEEPS, 2, ghost * groups, LANES), jnp.float32),
            pltpu.VMEM((2, freqs, nodes), jnp.float32),
            pltpu.SemaphoreType.DMA((SWEEPS, 2)),
            pltpu.SemaphoreType.DMA((SWEEPS, 2)),
            pltpu.SemaphoreType.DMA((2,)),
            pltpu.SemaphoreType.DMA((2,)),
        ],
        compiler_params=pltpu.CompilerParams(
            collective_id=0, has_side_effects=True, vmem_limit_bytes=62 * 1024 * 1024),
    )(action, edge_angle, edge_speed, neighbours, send_rows, refract_rate,
      refract_angle.reshape(1, nodes), shift_rate)


def solution(mesh):
    return jax.shard_map(
        shards,
        mesh=mesh,
        in_specs=(
            P("dir", None, "dom"),
            P(None, "dom"),
            P(None, "dom"),
            P(None, "dom"),
            P(None, "dom"),
            P(None, "dom"),
            P("dom"),
            P(None, "dom"),
        ),
        out_specs=P("dir", None, "dom"),
        check_vma=False,
    )
```

```python
import functools
import math

import jax
import jax.numpy as jnp
from jax import lax
from jax.experimental import pallas as pl
from jax.experimental.pallas import tpu as pltpu
from jax.sharding import PartitionSpec as P

NDIR = 64
NEIGH = 6
SWEEPS = 3
LANES = 128
MESH = pl.DeviceIdType.MESH
UNROLL = 8
BATCH = 32


def kernel(
    sizes, action_hbm, edge_angle_hbm, edge_speed_hbm, neighbours_hbm, send_rows_hbm, refract_rate_hbm,
    refract_angle_hbm, shift_rate_hbm, out,
    action, edge_angle, edge_speed, neighbours, send_rows, refract_rate, refract_angle, shift_rate,
    shared, slots, table, in_sem, f0, f1, f2, f3, scaled, weights, columns, swept, bearing, sends, halo,
    send_sem, recv_sem, dir_send, dir_recv,
):
    sector, freqs, nodes, ghost, groups, n_dom, n_dir = sizes
    fields = (f0, f1, f2, f3)
    dom = lax.axis_index("dom")
    here = lax.axis_index("dir")
    has_lower = dom > 0
    has_upper = dom < n_dom - 1
    next_dir = lax.rem(here + 1, n_dir)
    prev_dir = lax.rem(here + n_dir - 1, n_dir)

    loads = [
        pltpu.make_async_copy(source, target, in_sem.at[at]) for at, (source, target) in enumerate((
            (send_rows_hbm, send_rows), (neighbours_hbm, neighbours), (edge_angle_hbm, edge_angle),
            (edge_speed_hbm, edge_speed), (refract_angle_hbm, refract_angle),
            (refract_rate_hbm, refract_rate), (shift_rate_hbm, shift_rate), (neighbours_hbm, shared)))]
    planes = [
        pltpu.make_async_copy(
            action_hbm.at[:, pl.ds(group * 8, 8), :], action.at[:, pl.ds(group * 8, 8), :], in_sem.at[9 + group])
        for group in range(groups)]
    for load in loads[:2] + planes + loads[2:]:
        load.start()

    barrier = pltpu.get_barrier_semaphore()
    for other in (next_dir, prev_dir):
        pl.semaphore_signal(barrier, inc=1, device_id=(dom, other), device_id_type=MESH)

    @pl.when(has_lower)
    def _():
        pl.semaphore_signal(barrier, inc=1, device_id=(dom - 1, here), device_id_type=MESH)

    @pl.when(has_upper)
    def _():
        pl.semaphore_signal(barrier, inc=1, device_id=(dom + 1, here), device_id_type=MESH)

    low_at, high_at, width = nodes * groups, (nodes + ghost) * groups, ghost * groups

    @pl.when(dom == 0)
    def _():
        for field in (f0, f1, f2):
            field[pl.ds(low_at, width), :] = jnp.zeros((width, LANES), jnp.float32)

    @pl.when(dom == n_dom - 1)
    def _():
        for field in (f0, f1, f2):
            field[pl.ds(high_at, width), :] = jnp.zeros((width, LANES), jnp.float32)

    def to_lower(sweep):
        return pltpu.make_async_remote_copy(
            src_ref=sends.at[sweep, 0], dst_ref=fields[sweep].at[pl.ds(high_at, width)],
            send_sem=send_sem.at[sweep, 0], recv_sem=recv_sem.at[sweep, 0],
            device_id=(dom - 1, here), device_id_type=MESH)

    def to_upper(sweep):
        return pltpu.make_async_remote_copy(
            src_ref=sends.at[sweep, 1], dst_ref=fields[sweep].at[pl.ds(low_at, width)],
            send_sem=send_sem.at[sweep, 1], recv_sem=recv_sem.at[sweep, 1],
            device_id=(dom + 1, here), device_id_type=MESH)

    def start(sweep):
        @pl.when(has_lower)
        def _():
            to_lower(sweep).start()

        @pl.when(has_upper)
        def _():
            to_upper(sweep).start()

    def arrived(sweep):
        @pl.when(has_lower)
        def _():
            to_upper(sweep).wait_recv()

        @pl.when(has_upper)
        def _():
            to_lower(sweep).wait_recv()

    loads[1].wait()
    slots[...] = jnp.zeros_like(slots)
    for step in range(nodes // BATCH):
        slots[step * 8:step * 8 + NEIGH, :BATCH] = neighbours[:, step * BATCH:(step + 1) * BATCH] * groups
    to_table = pltpu.make_async_copy(slots, table, in_sem.at[8])
    to_table.start()
    for group in range(groups):
        planes[group].wait()
        for tile in range(nodes // LANES):
            block = action[:, group * 8:(group + 1) * 8, tile * LANES:(tile + 1) * LANES]
            turned = block.reshape(LANES, LANES).T
            f0[pl.ds(tile * LANES * groups + group, LANES, stride=groups), :] = turned
            scaled[pl.ds(tile * LANES * groups + group, LANES, stride=groups), :] = turned

    loads[0].wait()

    @pl.loop(0, ghost // UNROLL)
    def _(step):
        picked = [
            scaled[pl.ds(send_rows[side, step * UNROLL + u] * groups, groups), :]
            for u in range(UNROLL) for side in range(2)]
        for u in range(UNROLL):
            for side in range(2):
                sends[0, side, pl.ds((step * UNROLL + u) * groups, groups), :] = picked[2 * u + side]

    pl.semaphore_wait(barrier, 2 + has_lower.astype(jnp.int32) + has_upper.astype(jnp.int32))
    start(0)

    for load in loads[2:]:
        load.wait()
    first_dir = here * sector
    turn = 2.0 * math.pi / NDIR
    lane_dir = first_dir + lax.broadcasted_iota(jnp.int32, (8, LANES), 1) // 8
    lane_angle = lane_dir.astype(jnp.float32) * turn
    lane_cos, lane_sin = jnp.cos(lane_angle)[:1], jnp.sin(lane_angle)[:1]
    row_dir = first_dir + lax.broadcasted_iota(jnp.int32, (sector, nodes), 0)
    turned = jnp.sin(row_dir.astype(jnp.float32) * turn - refract_angle[...])
    for d in range(sector):
        bearing[d] = turned[d:d + 1]
    gap = jnp.zeros((8 - NEIGH, nodes), jnp.float32)
    edge_cos = edge_speed[...] * jnp.cos(edge_angle[...])
    edge_sin = edge_speed[...] * jnp.sin(edge_angle[...])
    parts = jnp.concatenate([edge_cos, gap, edge_sin, gap], axis=0)
    columns[...] = parts.T

    rows = 32

    @pl.loop(0, nodes // rows)
    def _(step):
        at = pl.multiple_of(step * rows, rows)
        block = columns[pl.ds(at, rows), :]
        places = [pl.ds(at * groups + group, rows, stride=groups) for group in range(groups)]
        base = [scaled[place, :] for place in places]
        found = []
        total = jnp.ones((rows, LANES), jnp.float32)
        for slot in range(NEIGH):
            weight = jnp.maximum(block[:, slot:slot + 1] * lane_cos + block[:, 8 + slot:9 + slot] * lane_sin, 0.0)
            found.append(weight)
            total = total + weight
        inverse = 1.0 / total
        for slot in range(NEIGH):
            weights[pl.ds(slot * nodes + at, rows), :] = found[slot] * inverse
        for group in range(groups):
            scaled[places[group], :] = base[group] * inverse

    to_table.wait()

    def update(field, start_row, weight_row, extra, row_of):
        total = scaled[pl.ds(start_row, groups), :]
        for slot in range(NEIGH):
            picked = field[pl.ds(row_of(slot), groups), :]
            total = total + weights[pl.ds(weight_row + (slot * nodes + extra), 1), :] * picked
        return total

    for sweep in range(SWEEPS):
        field, result = fields[sweep], fields[sweep + 1]
        arrived(sweep)
        if sweep < SWEEPS - 1:
            @pl.loop(0, ghost // UNROLL)
            def _(step):
                totals = []
                for u in range(UNROLL):
                    for side in range(2):
                        node = send_rows[side, step * UNROLL + u]
                        totals.append(update(
                            field, node * groups, node, 0, lambda slot, node=node: shared[slot, node] * groups))
                for u in range(UNROLL):
                    for side in range(2):
                        sends[sweep + 1, side, pl.ds((step * UNROLL + u) * groups, groups), :] = totals[2 * u + side]

            start(sweep + 1)

        @pl.loop(0, nodes // BATCH)
        def _(step):
            first = step * BATCH
            first_row = step * (BATCH * groups)
            first_slot = step * 8
            totals = []
            for u in range(BATCH):
                totals.append(update(
                    field, first_row + u * groups, first, u, lambda slot, u=u: table[first_slot + slot, u]))
            for u in range(BATCH):
                result[pl.ds(first_row + u * groups, groups), :] = totals[u]

    for tile in range(nodes // LANES):
        for group in range(groups):
            block = f3[pl.ds(tile * LANES * groups + group, LANES, stride=groups), :].T
            swept[:, group * 8:(group + 1) * 8, tile * LANES:(tile + 1) * LANES] = block.reshape(sector, 8, LANES)

    up = pltpu.make_async_remote_copy(
        src_ref=swept.at[sector - 1], dst_ref=halo.at[0], send_sem=dir_send.at[0], recv_sem=dir_recv.at[0],
        device_id=(dom, next_dir), device_id_type=MESH)
    down = pltpu.make_async_remote_copy(
        src_ref=swept.at[0], dst_ref=halo.at[1], send_sem=dir_send.at[1], recv_sem=dir_recv.at[1],
        device_id=(dom, prev_dir), device_id_type=MESH)
    up.start()
    down.start()

    freq = lax.broadcasted_iota(jnp.int32, (freqs, LANES), 0)

    def finish(d, before, after):
        places = [pl.ds(tile * LANES, LANES) for tile in range(nodes // LANES)]
        found = []
        for at in places:
            own = swept[d, :, at]
            speed = refract_rate[:, at] * bearing[d, :, at]
            refracted = own - (jnp.maximum(speed, 0.0) * (own - before(at)) + jnp.minimum(speed, 0.0) * (after(at) - own))
            lower = jnp.where(freq == 0, 0.0, pltpu.roll(refracted, 1, 0))
            upper = jnp.where(freq == freqs - 1, 0.0, pltpu.roll(refracted, freqs - 1, 0))
            rate = shift_rate[:, at]
            found.append(refracted - (
                jnp.maximum(rate, 0.0) * (refracted - lower) + jnp.minimum(rate, 0.0) * (upper - refracted)))
        for at, value in zip(places, found):
            out[d, :, at] = value

    @pl.loop(1, sector - 1)
    def _(d):
        finish(d, lambda at: swept[d - 1, :, at], lambda at: swept[d + 1, :, at])

    up.wait()
    finish(0, lambda at: halo[0, :, at], lambda at: swept[1, :, at])
    down.wait()
    finish(sector - 1, lambda at: swept[sector - 2, :, at], lambda at: halo[1, :, at])

    for sweep in range(SWEEPS):
        @pl.when(has_lower)
        def _():
            to_lower(sweep).wait_send()

        @pl.when(has_upper)
        def _():
            to_upper(sweep).wait_send()


def shards(
    action, edge_angle, edge_speed, neighbours, send_rows, refract_rate, refract_angle, shift_rate
):
    sector, freqs, nodes = action.shape
    ghost = send_rows.shape[1]
    groups = freqs // 8
    sizes = (sector, freqs, nodes, ghost, groups, lax.axis_size("dom"), lax.axis_size("dir"))
    field = pltpu.VMEM(((nodes + 2 * ghost) * groups, LANES), jnp.float32)
    local = pltpu.VMEM((nodes * groups, LANES), jnp.float32)
    return pl.pallas_call(
        functools.partial(kernel, sizes),
        out_shape=pltpu.VMEM(action.shape, jnp.float32),
        in_specs=[pl.BlockSpec(memory_space=pltpu.HBM)] * 8,
        out_specs=pl.BlockSpec(memory_space=pltpu.VMEM),
        scratch_shapes=[
            pltpu.VMEM(action.shape, jnp.float32),
            pltpu.VMEM(edge_angle.shape, jnp.float32),
            pltpu.VMEM(edge_speed.shape, jnp.float32),
            pltpu.VMEM(neighbours.shape, jnp.int32),
            pltpu.SMEM(send_rows.shape, jnp.int32),
            pltpu.VMEM(refract_rate.shape, jnp.float32),
            pltpu.VMEM((1, nodes), jnp.float32),
            pltpu.VMEM(shift_rate.shape, jnp.float32),
            pltpu.SMEM(neighbours.shape, jnp.int32),
            pltpu.VMEM((nodes // BATCH * 8, LANES), jnp.int32),
            pltpu.SMEM((nodes // BATCH * 8, LANES), jnp.int32),
            pltpu.SemaphoreType.DMA((9 + groups,)),
            field, field, field, local, local,
            pltpu.VMEM((NEIGH * nodes, LANES), jnp.float32),
            pltpu.VMEM((nodes, 16), jnp.float32),
            pltpu.VMEM((sector, freqs, nodes), jnp.float32),
            pltpu.VMEM((sector, 1, nodes), jnp.float32),
            pltpu.VMEM((SWEEPS, 2, ghost * groups, LANES), jnp.float32),
            pltpu.VMEM((2, freqs, nodes), jnp.float32),
            pltpu.SemaphoreType.DMA((SWEEPS, 2)),
            pltpu.SemaphoreType.DMA((SWEEPS, 2)),
            pltpu.SemaphoreType.DMA((2,)),
            pltpu.SemaphoreType.DMA((2,)),
        ],
        compiler_params=pltpu.CompilerParams(
            collective_id=0, has_side_effects=True, vmem_limit_bytes=62 * 1024 * 1024),
    )(action, edge_angle, edge_speed, neighbours, send_rows, refract_rate,
      refract_angle.reshape(1, nodes), shift_rate)


def solution(mesh):
    return jax.shard_map(
        shards,
        mesh=mesh,
        in_specs=(
            P("dir", None, "dom"),
            P(None, "dom"),
            P(None, "dom"),
            P(None, "dom"),
            P(None, "dom"),
            P(None, "dom"),
            P("dom"),
            P(None, "dom"),
        ),
        out_specs=P("dir", None, "dom"),
        check_vma=False,
    )
```

```python
import functools
import math

import jax
import jax.numpy as jnp
from jax import lax
from jax.experimental import pallas as pl
from jax.experimental.pallas import tpu as pltpu
from jax.sharding import PartitionSpec as P

NDIR = 64
NEIGH = 6
SWEEPS = 3
LANES = 128
MESH = pl.DeviceIdType.MESH
UNROLL = 8
BATCH = 32


def kernel(
    sizes, action_hbm, edge_angle_hbm, edge_speed_hbm, neighbours_hbm, send_rows_hbm, refract_rate_hbm,
    refract_angle_hbm, shift_rate_hbm, out,
    action, edge_angle, edge_speed, neighbours, send_rows, refract_rate, refract_angle, shift_rate,
    shared, slots, table, in_sem, f0, f1, f2, f3, scaled, weights, columns, swept, bearing, sends, halo,
    send_sem, recv_sem, dir_send, dir_recv,
):
    sector, freqs, nodes, ghost, groups, n_dom, n_dir = sizes
    fields = (f0, f1, f2, f3)
    dom = lax.axis_index("dom")
    here = lax.axis_index("dir")
    has_lower = dom > 0
    has_upper = dom < n_dom - 1
    next_dir = lax.rem(here + 1, n_dir)
    prev_dir = lax.rem(here + n_dir - 1, n_dir)

    loads = [
        pltpu.make_async_copy(source, target, in_sem.at[at]) for at, (source, target) in enumerate((
            (send_rows_hbm, send_rows), (neighbours_hbm, neighbours), (edge_angle_hbm, edge_angle),
            (edge_speed_hbm, edge_speed), (refract_angle_hbm, refract_angle),
            (refract_rate_hbm, refract_rate), (shift_rate_hbm, shift_rate), (neighbours_hbm, shared)))]
    planes = [
        pltpu.make_async_copy(
            action_hbm.at[:, pl.ds(group * 8, 8), :], action.at[:, pl.ds(group * 8, 8), :], in_sem.at[9 + group])
        for group in range(groups)]
    for load in loads[:2] + planes + loads[2:]:
        load.start()

    barrier = pltpu.get_barrier_semaphore()
    for other in (next_dir, prev_dir):
        pl.semaphore_signal(barrier, inc=1, device_id=(dom, other), device_id_type=MESH)

    @pl.when(has_lower)
    def _():
        pl.semaphore_signal(barrier, inc=1, device_id=(dom - 1, here), device_id_type=MESH)

    @pl.when(has_upper)
    def _():
        pl.semaphore_signal(barrier, inc=1, device_id=(dom + 1, here), device_id_type=MESH)

    low_at, high_at, width = nodes * groups, (nodes + ghost) * groups, ghost * groups

    @pl.when(dom == 0)
    def _():
        for field in (f0, f1, f2):
            field[pl.ds(low_at, width), :] = jnp.zeros((width, LANES), jnp.float32)

    @pl.when(dom == n_dom - 1)
    def _():
        for field in (f0, f1, f2):
            field[pl.ds(high_at, width), :] = jnp.zeros((width, LANES), jnp.float32)

    def to_lower(sweep):
        return pltpu.make_async_remote_copy(
            src_ref=sends.at[sweep, 0], dst_ref=fields[sweep].at[pl.ds(high_at, width)],
            send_sem=send_sem.at[sweep, 0], recv_sem=recv_sem.at[sweep, 0],
            device_id=(dom - 1, here), device_id_type=MESH)

    def to_upper(sweep):
        return pltpu.make_async_remote_copy(
            src_ref=sends.at[sweep, 1], dst_ref=fields[sweep].at[pl.ds(low_at, width)],
            send_sem=send_sem.at[sweep, 1], recv_sem=recv_sem.at[sweep, 1],
            device_id=(dom + 1, here), device_id_type=MESH)

    def start(sweep):
        @pl.when(has_lower)
        def _():
            to_lower(sweep).start()

        @pl.when(has_upper)
        def _():
            to_upper(sweep).start()

    def arrived(sweep):
        @pl.when(has_lower)
        def _():
            to_upper(sweep).wait_recv()

        @pl.when(has_upper)
        def _():
            to_lower(sweep).wait_recv()

    loads[1].wait()
    slots[...] = jnp.zeros_like(slots)
    for step in range(nodes // BATCH):
        slots[step * 8:step * 8 + NEIGH, :BATCH] = neighbours[:, step * BATCH:(step + 1) * BATCH] * groups
    to_table = pltpu.make_async_copy(slots, table, in_sem.at[8])
    to_table.start()
    for group in range(groups):
        planes[group].wait()
        for tile in range(nodes // LANES):
            block = action[:, group * 8:(group + 1) * 8, tile * LANES:(tile + 1) * LANES]
            turned = block.reshape(LANES, LANES).T
            f0[pl.ds(tile * LANES * groups + group, LANES, stride=groups), :] = turned
            scaled[pl.ds(tile * LANES * groups + group, LANES, stride=groups), :] = turned

    loads[0].wait()

    @pl.loop(0, ghost // UNROLL)
    def _(step):
        picked = [
            scaled[pl.ds(send_rows[side, step * UNROLL + u] * groups, groups), :]
            for u in range(UNROLL) for side in range(2)]
        for u in range(UNROLL):
            for side in range(2):
                sends[0, side, pl.ds((step * UNROLL + u) * groups, groups), :] = picked[2 * u + side]

    pl.semaphore_wait(barrier, 2 + has_lower.astype(jnp.int32) + has_upper.astype(jnp.int32))
    start(0)

    for load in loads[2:]:
        load.wait()
    first_dir = here * sector
    turn = 2.0 * math.pi / NDIR
    lane_dir = first_dir + lax.broadcasted_iota(jnp.int32, (8, LANES), 1) // 8
    lane_angle = lane_dir.astype(jnp.float32) * turn
    lane_cos, lane_sin = jnp.cos(lane_angle)[:1], jnp.sin(lane_angle)[:1]
    row_dir = first_dir + lax.broadcasted_iota(jnp.int32, (sector, nodes), 0)
    turned = jnp.sin(row_dir.astype(jnp.float32) * turn - refract_angle[...])
    for d in range(sector):
        bearing[d] = turned[d:d + 1]
    gap = jnp.zeros((8 - NEIGH, nodes), jnp.float32)
    edge_cos = edge_speed[...] * jnp.cos(edge_angle[...])
    edge_sin = edge_speed[...] * jnp.sin(edge_angle[...])
    parts = jnp.concatenate([edge_cos, gap, edge_sin, gap], axis=0)
    columns[...] = parts.T

    rows = 32

    @pl.loop(0, nodes // rows)
    def _(step):
        at = pl.multiple_of(step * rows, rows)
        block = columns[pl.ds(at, rows), :]
        places = [pl.ds(at * groups + group, rows, stride=groups) for group in range(groups)]
        base = [scaled[place, :] for place in places]
        found = []
        total = jnp.ones((rows, LANES), jnp.float32)
        for slot in range(NEIGH):
            weight = jnp.maximum(block[:, slot:slot + 1] * lane_cos + block[:, 8 + slot:9 + slot] * lane_sin, 0.0)
            found.append(weight)
            total = total + weight
        inverse = 1.0 / total
        for slot in range(NEIGH):
            weights[pl.ds(slot * nodes + at, rows), :] = found[slot] * inverse
        for group in range(groups):
            scaled[places[group], :] = base[group] * inverse

    to_table.wait()

    def update(field, start_row, weight_row, extra, row_of):
        total = scaled[pl.ds(start_row, groups), :]
        for slot in range(NEIGH):
            picked = field[pl.ds(row_of(slot), groups), :]
            total = total + weights[pl.ds(weight_row + (slot * nodes + extra), 1), :] * picked
        return total

    def to_next(tile):
        at = pl.ds(pl.multiple_of(tile * LANES, LANES), LANES)
        return pltpu.make_async_remote_copy(
            src_ref=swept.at[sector - 1, :, at], dst_ref=halo.at[0, :, at],
            send_sem=dir_send.at[0, tile], recv_sem=dir_recv.at[0, tile],
            device_id=(dom, next_dir), device_id_type=MESH)

    def to_prev(tile):
        at = pl.ds(pl.multiple_of(tile * LANES, LANES), LANES)
        return pltpu.make_async_remote_copy(
            src_ref=swept.at[0, :, at], dst_ref=halo.at[1, :, at],
            send_sem=dir_send.at[1, tile], recv_sem=dir_recv.at[1, tile],
            device_id=(dom, prev_dir), device_id_type=MESH)

    for sweep in range(SWEEPS):
        field, result = fields[sweep], fields[sweep + 1]
        arrived(sweep)
        if sweep < SWEEPS - 1:
            @pl.loop(0, ghost // UNROLL)
            def _(step):
                totals = []
                for u in range(UNROLL):
                    for side in range(2):
                        node = send_rows[side, step * UNROLL + u]
                        totals.append(update(
                            field, node * groups, node, 0, lambda slot, node=node: shared[slot, node] * groups))
                for u in range(UNROLL):
                    for side in range(2):
                        sends[sweep + 1, side, pl.ds((step * UNROLL + u) * groups, groups), :] = totals[2 * u + side]

            start(sweep + 1)

        def batches(step):
            first = step * BATCH
            first_row = step * (BATCH * groups)
            first_slot = step * 8
            totals = []
            for u in range(BATCH):
                totals.append(update(
                    field, first_row + u * groups, first, u, lambda slot, u=u: table[first_slot + slot, u]))
            for u in range(BATCH):
                result[pl.ds(first_row + u * groups, groups), :] = totals[u]

        if sweep < SWEEPS - 1:
            pl.loop(0, nodes // BATCH)(batches)
        else:
            @pl.loop(0, nodes // LANES)
            def _(tile):
                @pl.loop(0, LANES // BATCH)
                def _(step):
                    batches(tile * (LANES // BATCH) + step)

                at = pl.ds(pl.multiple_of(tile * LANES, LANES), LANES)
                blocks = [
                    result[pl.ds(tile * (LANES * groups) + group, LANES, stride=groups), :].T
                    for group in range(groups)]
                for group in range(groups):
                    swept[:, group * 8:(group + 1) * 8, at] = blocks[group].reshape(sector, 8, LANES)
                to_next(tile).start()
                to_prev(tile).start()

    freq = lax.broadcasted_iota(jnp.int32, (freqs, LANES), 0)

    def finish(d, before, after):
        places = [pl.ds(tile * LANES, LANES) for tile in range(nodes // LANES)]
        found = []
        for at in places:
            own = swept[d, :, at]
            speed = refract_rate[:, at] * bearing[d, :, at]
            refracted = own - (jnp.maximum(speed, 0.0) * (own - before(at)) + jnp.minimum(speed, 0.0) * (after(at) - own))
            lower = jnp.where(freq == 0, 0.0, pltpu.roll(refracted, 1, 0))
            upper = jnp.where(freq == freqs - 1, 0.0, pltpu.roll(refracted, freqs - 1, 0))
            rate = shift_rate[:, at]
            found.append(refracted - (
                jnp.maximum(rate, 0.0) * (refracted - lower) + jnp.minimum(rate, 0.0) * (upper - refracted)))
        for at, value in zip(places, found):
            out[d, :, at] = value

    @pl.loop(1, sector - 1)
    def _(d):
        finish(d, lambda at: swept[d - 1, :, at], lambda at: swept[d + 1, :, at])

    for tile in range(nodes // LANES):
        to_next(tile).wait()
    finish(0, lambda at: halo[0, :, at], lambda at: swept[1, :, at])
    for tile in range(nodes // LANES):
        to_prev(tile).wait()
    finish(sector - 1, lambda at: swept[sector - 2, :, at], lambda at: halo[1, :, at])

    for sweep in range(SWEEPS):
        @pl.when(has_lower)
        def _():
            to_lower(sweep).wait_send()

        @pl.when(has_upper)
        def _():
            to_upper(sweep).wait_send()


def shards(
    action, edge_angle, edge_speed, neighbours, send_rows, refract_rate, refract_angle, shift_rate
):
    sector, freqs, nodes = action.shape
    ghost = send_rows.shape[1]
    groups = freqs // 8
    sizes = (sector, freqs, nodes, ghost, groups, lax.axis_size("dom"), lax.axis_size("dir"))
    field = pltpu.VMEM(((nodes + 2 * ghost) * groups, LANES), jnp.float32)
    local = pltpu.VMEM((nodes * groups, LANES), jnp.float32)
    return pl.pallas_call(
        functools.partial(kernel, sizes),
        out_shape=pltpu.VMEM(action.shape, jnp.float32),
        in_specs=[pl.BlockSpec(memory_space=pltpu.HBM)] * 8,
        out_specs=pl.BlockSpec(memory_space=pltpu.VMEM),
        scratch_shapes=[
            pltpu.VMEM(action.shape, jnp.float32),
            pltpu.VMEM(edge_angle.shape, jnp.float32),
            pltpu.VMEM(edge_speed.shape, jnp.float32),
            pltpu.VMEM(neighbours.shape, jnp.int32),
            pltpu.SMEM(send_rows.shape, jnp.int32),
            pltpu.VMEM(refract_rate.shape, jnp.float32),
            pltpu.VMEM((1, nodes), jnp.float32),
            pltpu.VMEM(shift_rate.shape, jnp.float32),
            pltpu.SMEM(neighbours.shape, jnp.int32),
            pltpu.VMEM((nodes // BATCH * 8, LANES), jnp.int32),
            pltpu.SMEM((nodes // BATCH * 8, LANES), jnp.int32),
            pltpu.SemaphoreType.DMA((9 + groups,)),
            field, field, field, local, local,
            pltpu.VMEM((NEIGH * nodes, LANES), jnp.float32),
            pltpu.VMEM((nodes, 16), jnp.float32),
            pltpu.VMEM((sector, freqs, nodes), jnp.float32),
            pltpu.VMEM((sector, 1, nodes), jnp.float32),
            pltpu.VMEM((SWEEPS, 2, ghost * groups, LANES), jnp.float32),
            pltpu.VMEM((2, freqs, nodes), jnp.float32),
            pltpu.SemaphoreType.DMA((SWEEPS, 2)),
            pltpu.SemaphoreType.DMA((SWEEPS, 2)),
            pltpu.SemaphoreType.DMA((2, nodes // LANES)),
            pltpu.SemaphoreType.DMA((2, nodes // LANES)),
        ],
        compiler_params=pltpu.CompilerParams(
            collective_id=0, has_side_effects=True, vmem_limit_bytes=62 * 1024 * 1024),
    )(action, edge_angle, edge_speed, neighbours, send_rows, refract_rate,
      refract_angle.reshape(1, nodes), shift_rate)


def solution(mesh):
    return jax.shard_map(
        shards,
        mesh=mesh,
        in_specs=(
            P("dir", None, "dom"),
            P(None, "dom"),
            P(None, "dom"),
            P(None, "dom"),
            P(None, "dom"),
            P(None, "dom"),
            P("dom"),
            P(None, "dom"),
        ),
        out_specs=P("dir", None, "dom"),
        check_vma=False,
    )
```

```python
import functools
import math

import jax
import jax.numpy as jnp
from jax import lax
from jax.experimental import pallas as pl
from jax.experimental.pallas import tpu as pltpu
from jax.sharding import PartitionSpec as P

NDIR = 64
NEIGH = 6
SWEEPS = 3
LANES = 128
MESH = pl.DeviceIdType.MESH
UNROLL = 8
BATCH = 64
HALF = 32


def kernel(
    sizes, action_hbm, edge_angle_hbm, edge_speed_hbm, neighbours_hbm, send_rows_hbm, refract_rate_hbm,
    refract_angle_hbm, shift_rate_hbm, out,
    action, edge_angle, edge_speed, neighbours, send_rows, refract_rate, refract_angle, shift_rate,
    shared, slots, table, in_sem, f0, f1, f2, f3, scaled, weights, columns, swept, bearing, sends, halo,
    send_sem, recv_sem, dir_send, dir_recv,
):
    sector, freqs, nodes, ghost, groups, n_dom, n_dir = sizes
    fields = (f0, f1, f2, f3)
    dom = lax.axis_index("dom")
    here = lax.axis_index("dir")
    has_lower = dom > 0
    has_upper = dom < n_dom - 1
    next_dir = lax.rem(here + 1, n_dir)
    prev_dir = lax.rem(here + n_dir - 1, n_dir)

    loads = [
        pltpu.make_async_copy(source, target, in_sem.at[at]) for at, (source, target) in enumerate((
            (send_rows_hbm, send_rows), (neighbours_hbm, neighbours), (edge_angle_hbm, edge_angle),
            (edge_speed_hbm, edge_speed), (refract_angle_hbm, refract_angle),
            (refract_rate_hbm, refract_rate), (shift_rate_hbm, shift_rate), (neighbours_hbm, shared)))]
    planes = [
        pltpu.make_async_copy(
            action_hbm.at[:, pl.ds(group * 8, 8), :], action.at[:, pl.ds(group * 8, 8), :], in_sem.at[9 + group])
        for group in range(groups)]
    for load in loads[:2] + planes + loads[2:]:
        load.start()

    barrier = pltpu.get_barrier_semaphore()
    for other in (next_dir, prev_dir):
        pl.semaphore_signal(barrier, inc=1, device_id=(dom, other), device_id_type=MESH)

    @pl.when(has_lower)
    def _():
        pl.semaphore_signal(barrier, inc=1, device_id=(dom - 1, here), device_id_type=MESH)

    @pl.when(has_upper)
    def _():
        pl.semaphore_signal(barrier, inc=1, device_id=(dom + 1, here), device_id_type=MESH)

    low_at, high_at, width = nodes * groups, (nodes + ghost) * groups, ghost * groups

    @pl.when(dom == 0)
    def _():
        for field in (f0, f1, f2):
            field[pl.ds(low_at, width), :] = jnp.zeros((width, LANES), jnp.float32)

    @pl.when(dom == n_dom - 1)
    def _():
        for field in (f0, f1, f2):
            field[pl.ds(high_at, width), :] = jnp.zeros((width, LANES), jnp.float32)

    def to_lower(sweep):
        return pltpu.make_async_remote_copy(
            src_ref=sends.at[sweep, 0], dst_ref=fields[sweep].at[pl.ds(high_at, width)],
            send_sem=send_sem.at[sweep, 0], recv_sem=recv_sem.at[sweep, 0],
            device_id=(dom - 1, here), device_id_type=MESH)

    def to_upper(sweep):
        return pltpu.make_async_remote_copy(
            src_ref=sends.at[sweep, 1], dst_ref=fields[sweep].at[pl.ds(low_at, width)],
            send_sem=send_sem.at[sweep, 1], recv_sem=recv_sem.at[sweep, 1],
            device_id=(dom + 1, here), device_id_type=MESH)

    def start(sweep):
        @pl.when(has_lower)
        def _():
            to_lower(sweep).start()

        @pl.when(has_upper)
        def _():
            to_upper(sweep).start()

    def arrived(sweep):
        @pl.when(has_lower)
        def _():
            to_upper(sweep).wait_recv()

        @pl.when(has_upper)
        def _():
            to_lower(sweep).wait_recv()

    loads[1].wait()
    slots[...] = jnp.zeros_like(slots)
    for step in range(nodes // BATCH):
        slots[step * 8:step * 8 + NEIGH, :BATCH] = neighbours[:, step * BATCH:(step + 1) * BATCH] * groups
    to_table = pltpu.make_async_copy(slots, table, in_sem.at[8])
    to_table.start()
    for load in loads[2:]:
        load.wait()
    first_dir = here * sector
    turn = 2.0 * math.pi / NDIR
    lane_dir = first_dir + lax.broadcasted_iota(jnp.int32, (8, LANES), 1) // 8
    lane_angle = lane_dir.astype(jnp.float32) * turn
    lane_cos, lane_sin = jnp.cos(lane_angle)[:1], jnp.sin(lane_angle)[:1]
    row_dir = first_dir + lax.broadcasted_iota(jnp.int32, (sector, nodes), 0)
    turned = jnp.sin(row_dir.astype(jnp.float32) * turn - refract_angle[...])
    for d in range(sector):
        bearing[d] = turned[d:d + 1]
    gap = jnp.zeros((8 - NEIGH, nodes), jnp.float32)
    edge_cos = edge_speed[...] * jnp.cos(edge_angle[...])
    edge_sin = edge_speed[...] * jnp.sin(edge_angle[...])
    parts = jnp.concatenate([edge_cos, gap, edge_sin, gap], axis=0)
    columns[...] = parts.T

    for group in range(groups):
        planes[group].wait()
        for tile in range(nodes // LANES):
            block = action[:, group * 8:(group + 1) * 8, tile * LANES:(tile + 1) * LANES]
            turned = block.reshape(LANES, LANES).T
            f0[pl.ds(tile * LANES * groups + group, LANES, stride=groups), :] = turned
            scaled[pl.ds(tile * LANES * groups + group, LANES, stride=groups), :] = turned

    loads[0].wait()

    @pl.loop(0, ghost // UNROLL)
    def _(step):
        picked = [
            scaled[pl.ds(send_rows[side, step * UNROLL + u] * groups, groups), :]
            for u in range(UNROLL) for side in range(2)]
        for u in range(UNROLL):
            for side in range(2):
                sends[0, side, pl.ds((step * UNROLL + u) * groups, groups), :] = picked[2 * u + side]

    pl.semaphore_wait(barrier, 2 + has_lower.astype(jnp.int32) + has_upper.astype(jnp.int32))
    start(0)

    rows = 32

    @pl.loop(0, nodes // rows)
    def _(step):
        at = pl.multiple_of(step * rows, rows)
        block = columns[pl.ds(at, rows), :]
        places = [pl.ds(at * groups + group, rows, stride=groups) for group in range(groups)]
        base = [scaled[place, :] for place in places]
        found = []
        total = jnp.ones((rows, LANES), jnp.float32)
        for slot in range(NEIGH):
            weight = jnp.maximum(block[:, slot:slot + 1] * lane_cos + block[:, 8 + slot:9 + slot] * lane_sin, 0.0)
            found.append(weight)
            total = total + weight
        inverse = 1.0 / total
        for slot in range(NEIGH):
            weights[pl.ds(slot * nodes + at, rows), :] = found[slot] * inverse
        for group in range(groups):
            scaled[places[group], :] = base[group] * inverse

    to_table.wait()

    def update(field, start_row, weight_row, extra, row_of):
        total = scaled[pl.ds(start_row, groups), :]
        for slot in range(NEIGH):
            picked = field[pl.ds(row_of(slot), groups), :]
            total = total + weights[pl.ds(weight_row + (slot * nodes + extra), 1), :] * picked
        return total

    def to_next(tile):
        at = pl.ds(pl.multiple_of(tile * LANES, LANES), LANES)
        return pltpu.make_async_remote_copy(
            src_ref=swept.at[sector - 1, :, at], dst_ref=halo.at[0, :, at],
            send_sem=dir_send.at[0, tile], recv_sem=dir_recv.at[0, tile],
            device_id=(dom, next_dir), device_id_type=MESH)

    def to_prev(tile):
        at = pl.ds(pl.multiple_of(tile * LANES, LANES), LANES)
        return pltpu.make_async_remote_copy(
            src_ref=swept.at[0, :, at], dst_ref=halo.at[1, :, at],
            send_sem=dir_send.at[1, tile], recv_sem=dir_recv.at[1, tile],
            device_id=(dom, prev_dir), device_id_type=MESH)

    for sweep in range(SWEEPS):
        field, result = fields[sweep], fields[sweep + 1]
        arrived(sweep)
        if sweep < SWEEPS - 1:
            @pl.loop(0, ghost // UNROLL)
            def _(step):
                totals = []
                for u in range(UNROLL):
                    for side in range(2):
                        node = send_rows[side, step * UNROLL + u]
                        totals.append(update(
                            field, node * groups, node, 0, lambda slot, node=node: shared[slot, node] * groups))
                for u in range(UNROLL):
                    for side in range(2):
                        sends[sweep + 1, side, pl.ds((step * UNROLL + u) * groups, groups), :] = totals[2 * u + side]

            start(sweep + 1)

        def batches(step):
            first = step * BATCH
            first_row = step * (BATCH * groups)
            first_slot = step * 8
            for half in range(0, BATCH, HALF):
                totals = []
                for u in range(half, half + HALF):
                    totals.append(update(
                        field, first_row + u * groups, first, u, lambda slot, u=u: table[first_slot + slot, u]))
                for u in range(half, half + HALF):
                    result[pl.ds(first_row + u * groups, groups), :] = totals[u - half]

        if sweep < SWEEPS - 1:
            pl.loop(0, nodes // BATCH)(batches)
        else:
            @pl.loop(0, nodes // LANES)
            def _(tile):
                @pl.loop(0, LANES // BATCH)
                def _(step):
                    batches(tile * (LANES // BATCH) + step)

                at = pl.ds(pl.multiple_of(tile * LANES, LANES), LANES)
                blocks = [
                    result[pl.ds(tile * (LANES * groups) + group, LANES, stride=groups), :].T
                    for group in range(groups)]
                for group in range(groups):
                    swept[:, group * 8:(group + 1) * 8, at] = blocks[group].reshape(sector, 8, LANES)
                to_next(tile).start()
                to_prev(tile).start()

    freq = lax.broadcasted_iota(jnp.int32, (freqs, LANES), 0)

    def finish(d, before, after):
        places = [pl.ds(tile * LANES, LANES) for tile in range(nodes // LANES)]
        found = []
        for at in places:
            own = swept[d, :, at]
            speed = refract_rate[:, at] * bearing[d, :, at]
            refracted = own - (jnp.maximum(speed, 0.0) * (own - before(at)) + jnp.minimum(speed, 0.0) * (after(at) - own))
            lower = jnp.where(freq == 0, 0.0, pltpu.roll(refracted, 1, 0))
            upper = jnp.where(freq == freqs - 1, 0.0, pltpu.roll(refracted, freqs - 1, 0))
            rate = shift_rate[:, at]
            found.append(refracted - (
                jnp.maximum(rate, 0.0) * (refracted - lower) + jnp.minimum(rate, 0.0) * (upper - refracted)))
        for at, value in zip(places, found):
            out[d, :, at] = value

    @pl.loop(1, sector - 1)
    def _(d):
        finish(d, lambda at: swept[d - 1, :, at], lambda at: swept[d + 1, :, at])

    for tile in range(nodes // LANES):
        to_next(tile).wait()
    finish(0, lambda at: halo[0, :, at], lambda at: swept[1, :, at])
    for tile in range(nodes // LANES):
        to_prev(tile).wait()
    finish(sector - 1, lambda at: swept[sector - 2, :, at], lambda at: halo[1, :, at])

    for sweep in range(SWEEPS):
        @pl.when(has_lower)
        def _():
            to_lower(sweep).wait_send()

        @pl.when(has_upper)
        def _():
            to_upper(sweep).wait_send()


def shards(
    action, edge_angle, edge_speed, neighbours, send_rows, refract_rate, refract_angle, shift_rate
):
    sector, freqs, nodes = action.shape
    ghost = send_rows.shape[1]
    groups = freqs // 8
    sizes = (sector, freqs, nodes, ghost, groups, lax.axis_size("dom"), lax.axis_size("dir"))
    field = pltpu.VMEM(((nodes + 2 * ghost) * groups, LANES), jnp.float32)
    local = pltpu.VMEM((nodes * groups, LANES), jnp.float32)
    return pl.pallas_call(
        functools.partial(kernel, sizes),
        out_shape=pltpu.VMEM(action.shape, jnp.float32),
        in_specs=[pl.BlockSpec(memory_space=pltpu.HBM)] * 8,
        out_specs=pl.BlockSpec(memory_space=pltpu.VMEM),
        scratch_shapes=[
            pltpu.VMEM(action.shape, jnp.float32),
            pltpu.VMEM(edge_angle.shape, jnp.float32),
            pltpu.VMEM(edge_speed.shape, jnp.float32),
            pltpu.VMEM(neighbours.shape, jnp.int32),
            pltpu.SMEM(send_rows.shape, jnp.int32),
            pltpu.VMEM(refract_rate.shape, jnp.float32),
            pltpu.VMEM((1, nodes), jnp.float32),
            pltpu.VMEM(shift_rate.shape, jnp.float32),
            pltpu.SMEM(neighbours.shape, jnp.int32),
            pltpu.VMEM((nodes // BATCH * 8, LANES), jnp.int32),
            pltpu.SMEM((nodes // BATCH * 8, LANES), jnp.int32),
            pltpu.SemaphoreType.DMA((9 + groups,)),
            field, field, field, local, local,
            pltpu.VMEM((NEIGH * nodes, LANES), jnp.float32),
            pltpu.VMEM((nodes, 16), jnp.float32),
            pltpu.VMEM((sector, freqs, nodes), jnp.float32),
            pltpu.VMEM((sector, 1, nodes), jnp.float32),
            pltpu.VMEM((SWEEPS, 2, ghost * groups, LANES), jnp.float32),
            pltpu.VMEM((2, freqs, nodes), jnp.float32),
            pltpu.SemaphoreType.DMA((SWEEPS, 2)),
            pltpu.SemaphoreType.DMA((SWEEPS, 2)),
            pltpu.SemaphoreType.DMA((2, nodes // LANES)),
            pltpu.SemaphoreType.DMA((2, nodes // LANES)),
        ],
        compiler_params=pltpu.CompilerParams(
            collective_id=0, has_side_effects=True, vmem_limit_bytes=62 * 1024 * 1024),
    )(action, edge_angle, edge_speed, neighbours, send_rows, refract_rate,
      refract_angle.reshape(1, nodes), shift_rate)


def solution(mesh):
    return jax.shard_map(
        shards,
        mesh=mesh,
        in_specs=(
            P("dir", None, "dom"),
            P(None, "dom"),
            P(None, "dom"),
            P(None, "dom"),
            P(None, "dom"),
            P(None, "dom"),
            P("dom"),
            P(None, "dom"),
        ),
        out_specs=P("dir", None, "dom"),
        check_vma=False,
    )
```

```python
import functools
import math

import jax
import jax.numpy as jnp
from jax import lax
from jax.experimental import pallas as pl
from jax.experimental.pallas import tpu as pltpu
from jax.sharding import PartitionSpec as P

NDIR = 64
NEIGH = 6
SWEEPS = 3
LANES = 128
MESH = pl.DeviceIdType.MESH
UNROLL = 8
BATCH = 32


def kernel(
    sizes, action_hbm, edge_angle_hbm, edge_speed_hbm, neighbours_hbm, send_rows_hbm, refract_rate_hbm,
    refract_angle_hbm, shift_rate_hbm, out,
    action, edge_angle, edge_speed, neighbours, send_rows, refract_rate, refract_angle, shift_rate,
    shared, slots, table, in_sem, f0, f1, f2, f3, scaled, weights, columns, swept, bearing, sends,
    send_sem, recv_sem, dir_send, dir_recv,
):
    sector, freqs, nodes, ghost, groups, n_dom, n_dir = sizes
    fields = (f0, f1, f2, f3)
    dom = lax.axis_index("dom")
    here = lax.axis_index("dir")
    has_lower = dom > 0
    has_upper = dom < n_dom - 1
    next_dir = lax.rem(here + 1, n_dir)
    prev_dir = lax.rem(here + n_dir - 1, n_dir)

    loads = [
        pltpu.make_async_copy(source, target, in_sem.at[at]) for at, (source, target) in enumerate((
            (send_rows_hbm, send_rows), (neighbours_hbm, neighbours), (edge_angle_hbm, edge_angle),
            (edge_speed_hbm, edge_speed), (refract_angle_hbm, refract_angle),
            (refract_rate_hbm, refract_rate), (shift_rate_hbm, shift_rate), (neighbours_hbm, shared)))]
    planes = [
        pltpu.make_async_copy(
            action_hbm.at[:, pl.ds(group * 8, 8), :], action.at[:, pl.ds(group * 8, 8), :], in_sem.at[9 + group])
        for group in range(groups)]
    for load in loads[:2] + planes + loads[2:]:
        load.start()

    barrier = pltpu.get_barrier_semaphore()
    for other in (next_dir, prev_dir):
        pl.semaphore_signal(barrier, inc=1, device_id=(dom, other), device_id_type=MESH)

    @pl.when(has_lower)
    def _():
        pl.semaphore_signal(barrier, inc=1, device_id=(dom - 1, here), device_id_type=MESH)

    @pl.when(has_upper)
    def _():
        pl.semaphore_signal(barrier, inc=1, device_id=(dom + 1, here), device_id_type=MESH)

    low_at, high_at, width = nodes * groups, (nodes + ghost) * groups, ghost * groups

    @pl.when(dom == 0)
    def _():
        for field in (f0, f1, f2):
            field[pl.ds(low_at, width), :] = jnp.zeros((width, LANES), jnp.float32)

    @pl.when(dom == n_dom - 1)
    def _():
        for field in (f0, f1, f2):
            field[pl.ds(high_at, width), :] = jnp.zeros((width, LANES), jnp.float32)

    def to_lower(sweep):
        return pltpu.make_async_remote_copy(
            src_ref=sends.at[sweep, 0], dst_ref=fields[sweep].at[pl.ds(high_at, width)],
            send_sem=send_sem.at[sweep, 0], recv_sem=recv_sem.at[sweep, 0],
            device_id=(dom - 1, here), device_id_type=MESH)

    def to_upper(sweep):
        return pltpu.make_async_remote_copy(
            src_ref=sends.at[sweep, 1], dst_ref=fields[sweep].at[pl.ds(low_at, width)],
            send_sem=send_sem.at[sweep, 1], recv_sem=recv_sem.at[sweep, 1],
            device_id=(dom + 1, here), device_id_type=MESH)

    def start(sweep):
        @pl.when(has_lower)
        def _():
            to_lower(sweep).start()

        @pl.when(has_upper)
        def _():
            to_upper(sweep).start()

    def arrived(sweep):
        @pl.when(has_lower)
        def _():
            to_upper(sweep).wait_recv()

        @pl.when(has_upper)
        def _():
            to_lower(sweep).wait_recv()

    loads[1].wait()
    slots[...] = jnp.zeros_like(slots)
    for step in range(nodes // BATCH):
        slots[step * 8:step * 8 + NEIGH, :BATCH] = neighbours[:, step * BATCH:(step + 1) * BATCH] * groups
    to_table = pltpu.make_async_copy(slots, table, in_sem.at[8])
    to_table.start()
    for group in range(groups):
        planes[group].wait()

    @pl.loop(0, nodes // LANES)
    def _(tile):
        at = pl.ds(pl.multiple_of(tile * LANES, LANES), LANES)
        blocks = [
            action[:, group * 8:(group + 1) * 8, at].reshape(LANES, LANES).T for group in range(groups)]
        for group in range(groups):
            where = pl.ds(tile * (LANES * groups) + group, LANES, stride=groups)
            f0[where, :] = blocks[group]
            scaled[where, :] = blocks[group]

    loads[0].wait()

    @pl.loop(0, ghost // UNROLL)
    def _(step):
        picked = [
            scaled[pl.ds(send_rows[side, step * UNROLL + u] * groups, groups), :]
            for u in range(UNROLL) for side in range(2)]
        for u in range(UNROLL):
            for side in range(2):
                sends[0, side, pl.ds((step * UNROLL + u) * groups, groups), :] = picked[2 * u + side]

    pl.semaphore_wait(barrier, 2 + has_lower.astype(jnp.int32) + has_upper.astype(jnp.int32))
    start(0)

    for load in loads[2:]:
        load.wait()
    first_dir = here * sector
    turn = 2.0 * math.pi / NDIR
    lane_dir = first_dir + lax.broadcasted_iota(jnp.int32, (8, LANES), 1) // 8
    lane_angle = lane_dir.astype(jnp.float32) * turn
    lane_cos, lane_sin = jnp.cos(lane_angle)[:1], jnp.sin(lane_angle)[:1]
    row_dir = first_dir + lax.broadcasted_iota(jnp.int32, (sector, nodes), 0)
    turned = jnp.sin(row_dir.astype(jnp.float32) * turn - refract_angle[...])
    for d in range(sector):
        bearing[d] = turned[d:d + 1]
    gap = jnp.zeros((8 - NEIGH, nodes), jnp.float32)
    edge_cos = edge_speed[...] * jnp.cos(edge_angle[...])
    edge_sin = edge_speed[...] * jnp.sin(edge_angle[...])
    parts = jnp.concatenate([edge_cos, gap, edge_sin, gap], axis=0)
    columns[...] = parts.T

    rows = 32

    @pl.loop(0, nodes // rows)
    def _(step):
        at = pl.multiple_of(step * rows, rows)
        block = columns[pl.ds(at, rows), :]
        places = [pl.ds(at * groups + group, rows, stride=groups) for group in range(groups)]
        base = [scaled[place, :] for place in places]
        found = []
        total = jnp.ones((rows, LANES), jnp.float32)
        for slot in range(NEIGH):
            weight = jnp.maximum(block[:, slot:slot + 1] * lane_cos + block[:, 8 + slot:9 + slot] * lane_sin, 0.0)
            found.append(weight)
            total = total + weight
        inverse = 1.0 / total
        for slot in range(NEIGH):
            weights[pl.ds(slot * nodes + at, rows), :] = found[slot] * inverse
        for group in range(groups):
            scaled[places[group], :] = base[group] * inverse

    to_table.wait()

    def update(field, start_row, weight_row, extra, row_of):
        total = scaled[pl.ds(start_row, groups), :]
        for slot in range(NEIGH):
            picked = field[pl.ds(row_of(slot), groups), :]
            total = total + weights[pl.ds(weight_row + (slot * nodes + extra), 1), :] * picked
        return total

    def to_next(tile):
        at = pl.ds(pl.multiple_of(tile * LANES, LANES), LANES)
        return pltpu.make_async_remote_copy(
            src_ref=swept.at[sector, :, at], dst_ref=swept.at[0, :, at],
            send_sem=dir_send.at[0, tile], recv_sem=dir_recv.at[0, tile],
            device_id=(dom, next_dir), device_id_type=MESH)

    def to_prev(tile):
        at = pl.ds(pl.multiple_of(tile * LANES, LANES), LANES)
        return pltpu.make_async_remote_copy(
            src_ref=swept.at[1, :, at], dst_ref=swept.at[sector + 1, :, at],
            send_sem=dir_send.at[1, tile], recv_sem=dir_recv.at[1, tile],
            device_id=(dom, prev_dir), device_id_type=MESH)

    for sweep in range(SWEEPS):
        field, result = fields[sweep], fields[sweep + 1]
        arrived(sweep)
        if sweep < SWEEPS - 1:
            @pl.loop(0, ghost // UNROLL)
            def _(step):
                totals = []
                for u in range(UNROLL):
                    for side in range(2):
                        node = send_rows[side, step * UNROLL + u]
                        totals.append(update(
                            field, node * groups, node, 0, lambda slot, node=node: shared[slot, node] * groups))
                for u in range(UNROLL):
                    for side in range(2):
                        sends[sweep + 1, side, pl.ds((step * UNROLL + u) * groups, groups), :] = totals[2 * u + side]

            start(sweep + 1)

        def batches(step):
            first = step * BATCH
            first_row = step * (BATCH * groups)
            first_slot = step * 8
            totals = []
            for u in range(BATCH):
                totals.append(update(
                    field, first_row + u * groups, first, u, lambda slot, u=u: table[first_slot + slot, u]))
            for u in range(BATCH):
                result[pl.ds(first_row + u * groups, groups), :] = totals[u]

        if sweep < SWEEPS - 1:
            pl.loop(0, nodes // BATCH)(batches)
        else:
            @pl.loop(0, nodes // LANES)
            def _(tile):
                @pl.loop(0, LANES // BATCH)
                def _(step):
                    batches(tile * (LANES // BATCH) + step)

                at = pl.ds(pl.multiple_of(tile * LANES, LANES), LANES)
                blocks = [
                    result[pl.ds(tile * (LANES * groups) + group, LANES, stride=groups), :].T
                    for group in range(groups)]
                for group in range(groups):
                    swept[1:sector + 1, group * 8:(group + 1) * 8, at] = blocks[group].reshape(sector, 8, LANES)
                to_next(tile).start()
                to_prev(tile).start()

    freq = lax.broadcasted_iota(jnp.int32, (freqs, LANES), 0)

    def finish(d):
        places = [pl.ds(tile * LANES, LANES) for tile in range(nodes // LANES)]
        found = []
        for at in places:
            own = swept[d + 1, :, at]
            speed = refract_rate[:, at] * bearing[d, :, at]
            refracted = own - (jnp.maximum(speed, 0.0) * (own - swept[d, :, at]) + jnp.minimum(speed, 0.0) * (swept[d + 2, :, at] - own))
            lower = jnp.where(freq == 0, 0.0, pltpu.roll(refracted, 1, 0))
            upper = jnp.where(freq == freqs - 1, 0.0, pltpu.roll(refracted, freqs - 1, 0))
            rate = shift_rate[:, at]
            found.append(refracted - (
                jnp.maximum(rate, 0.0) * (refracted - lower) + jnp.minimum(rate, 0.0) * (upper - refracted)))
        for at, value in zip(places, found):
            out[d, :, at] = value

    @pl.loop(0, sector)
    def _(step):
        @pl.when(step == sector - 2)
        def _():
            for tile in range(nodes // LANES):
                to_next(tile).wait()
                to_prev(tile).wait()

        finish(lax.rem(step + 1, sector))

    for sweep in range(SWEEPS):
        @pl.when(has_lower)
        def _():
            to_lower(sweep).wait_send()

        @pl.when(has_upper)
        def _():
            to_upper(sweep).wait_send()


def shards(
    action, edge_angle, edge_speed, neighbours, send_rows, refract_rate, refract_angle, shift_rate
):
    sector, freqs, nodes = action.shape
    ghost = send_rows.shape[1]
    groups = freqs // 8
    sizes = (sector, freqs, nodes, ghost, groups, lax.axis_size("dom"), lax.axis_size("dir"))
    field = pltpu.VMEM(((nodes + 2 * ghost) * groups, LANES), jnp.float32)
    local = pltpu.VMEM((nodes * groups, LANES), jnp.float32)
    return pl.pallas_call(
        functools.partial(kernel, sizes),
        out_shape=pltpu.VMEM(action.shape, jnp.float32),
        in_specs=[pl.BlockSpec(memory_space=pltpu.HBM)] * 8,
        out_specs=pl.BlockSpec(memory_space=pltpu.VMEM),
        scratch_shapes=[
            pltpu.VMEM(action.shape, jnp.float32),
            pltpu.VMEM(edge_angle.shape, jnp.float32),
            pltpu.VMEM(edge_speed.shape, jnp.float32),
            pltpu.VMEM(neighbours.shape, jnp.int32),
            pltpu.SMEM(send_rows.shape, jnp.int32),
            pltpu.VMEM(refract_rate.shape, jnp.float32),
            pltpu.VMEM((1, nodes), jnp.float32),
            pltpu.VMEM(shift_rate.shape, jnp.float32),
            pltpu.SMEM(neighbours.shape, jnp.int32),
            pltpu.VMEM((nodes // BATCH * 8, LANES), jnp.int32),
            pltpu.SMEM((nodes // BATCH * 8, LANES), jnp.int32),
            pltpu.SemaphoreType.DMA((9 + groups,)),
            field, field, field, local, local,
            pltpu.VMEM((NEIGH * nodes, LANES), jnp.float32),
            pltpu.VMEM((nodes, 16), jnp.float32),
            pltpu.VMEM((sector + 2, freqs, nodes), jnp.float32),
            pltpu.VMEM((sector, 1, nodes), jnp.float32),
            pltpu.VMEM((SWEEPS, 2, ghost * groups, LANES), jnp.float32),
            pltpu.SemaphoreType.DMA((SWEEPS, 2)),
            pltpu.SemaphoreType.DMA((SWEEPS, 2)),
            pltpu.SemaphoreType.DMA((2, nodes // LANES)),
            pltpu.SemaphoreType.DMA((2, nodes // LANES)),
        ],
        compiler_params=pltpu.CompilerParams(
            collective_id=0, has_side_effects=True, vmem_limit_bytes=62 * 1024 * 1024),
    )(action, edge_angle, edge_speed, neighbours, send_rows, refract_rate,
      refract_angle.reshape(1, nodes), shift_rate)


def solution(mesh):
    return jax.shard_map(
        shards,
        mesh=mesh,
        in_specs=(
            P("dir", None, "dom"),
            P(None, "dom"),
            P(None, "dom"),
            P(None, "dom"),
            P(None, "dom"),
            P(None, "dom"),
            P("dom"),
            P(None, "dom"),
        ),
        out_specs=P("dir", None, "dom"),
        check_vma=False,
    )
```

```python
import functools
import math

import jax
import jax.numpy as jnp
from jax import lax
from jax.experimental import pallas as pl
from jax.experimental.pallas import tpu as pltpu
from jax.sharding import PartitionSpec as P

NDIR = 64
NEIGH = 6
SWEEPS = 3
LANES = 128
MESH = pl.DeviceIdType.MESH
UNROLL = 8
BATCH = 32


def kernel(
    sizes, action_hbm, edge_angle_hbm, edge_speed_hbm, neighbours_hbm, send_rows_hbm, refract_rate_hbm,
    refract_angle_hbm, shift_rate_hbm, out,
    action, edge_angle, edge_speed, neighbours, send_rows, refract_rate, refract_angle, shift_rate,
    shared, slots, table, in_sem, f0, f1, f2, f3, scaled, weights, columns, swept, bearing, sends, halo,
    send_sem, recv_sem, dir_send, dir_recv,
):
    sector, freqs, nodes, ghost, groups, n_dom, n_dir = sizes
    fields = (f0, f1, f2, f3)
    dom = lax.axis_index("dom")
    here = lax.axis_index("dir")
    has_lower = dom > 0
    has_upper = dom < n_dom - 1
    next_dir = lax.rem(here + 1, n_dir)
    prev_dir = lax.rem(here + n_dir - 1, n_dir)

    loads = [
        pltpu.make_async_copy(source, target, in_sem.at[at]) for at, (source, target) in enumerate((
            (send_rows_hbm, send_rows), (neighbours_hbm, neighbours), (edge_angle_hbm, edge_angle),
            (edge_speed_hbm, edge_speed), (refract_angle_hbm, refract_angle),
            (refract_rate_hbm, refract_rate), (shift_rate_hbm, shift_rate), (neighbours_hbm, shared)))]
    planes = [
        pltpu.make_async_copy(
            action_hbm.at[:, pl.ds(group * 8, 8), :], action.at[:, pl.ds(group * 8, 8), :], in_sem.at[9 + group])
        for group in range(groups)]
    for load in loads[:2] + planes + loads[2:]:
        load.start()

    barrier = pltpu.get_barrier_semaphore()
    for other in (next_dir, prev_dir):
        pl.semaphore_signal(barrier, inc=1, device_id=(dom, other), device_id_type=MESH)

    @pl.when(has_lower)
    def _():
        pl.semaphore_signal(barrier, inc=1, device_id=(dom - 1, here), device_id_type=MESH)

    @pl.when(has_upper)
    def _():
        pl.semaphore_signal(barrier, inc=1, device_id=(dom + 1, here), device_id_type=MESH)

    low_at, high_at, width = nodes * groups, (nodes + ghost) * groups, ghost * groups

    @pl.when(dom == 0)
    def _():
        for field in (f0, f1, f2):
            field[pl.ds(low_at, width), :] = jnp.zeros((width, LANES), jnp.float32)

    @pl.when(dom == n_dom - 1)
    def _():
        for field in (f0, f1, f2):
            field[pl.ds(high_at, width), :] = jnp.zeros((width, LANES), jnp.float32)

    def to_lower(sweep):
        return pltpu.make_async_remote_copy(
            src_ref=sends.at[sweep, 0], dst_ref=fields[sweep].at[pl.ds(high_at, width)],
            send_sem=send_sem.at[sweep, 0], recv_sem=recv_sem.at[sweep, 0],
            device_id=(dom - 1, here), device_id_type=MESH)

    def to_upper(sweep):
        return pltpu.make_async_remote_copy(
            src_ref=sends.at[sweep, 1], dst_ref=fields[sweep].at[pl.ds(low_at, width)],
            send_sem=send_sem.at[sweep, 1], recv_sem=recv_sem.at[sweep, 1],
            device_id=(dom + 1, here), device_id_type=MESH)

    def start(sweep):
        @pl.when(has_lower)
        def _():
            to_lower(sweep).start()

        @pl.when(has_upper)
        def _():
            to_upper(sweep).start()

    def arrived(sweep):
        @pl.when(has_lower)
        def _():
            to_upper(sweep).wait_recv()

        @pl.when(has_upper)
        def _():
            to_lower(sweep).wait_recv()

    loads[1].wait()
    slots[...] = jnp.zeros_like(slots)
    for step in range(nodes // BATCH):
        slots[step * 8:step * 8 + NEIGH, :BATCH] = neighbours[:, step * BATCH:(step + 1) * BATCH] * groups
    to_table = pltpu.make_async_copy(slots, table, in_sem.at[8])
    to_table.start()
    for group in range(groups):
        planes[group].wait()
        for tile in range(nodes // LANES):
            block = action[:, group * 8:(group + 1) * 8, tile * LANES:(tile + 1) * LANES]
            turned = block.reshape(LANES, LANES).T
            scaled[pl.ds(tile * LANES * groups + group, LANES, stride=groups), :] = turned

    loads[0].wait()

    @pl.loop(0, ghost // UNROLL)
    def _(step):
        picked = [
            scaled[pl.ds(send_rows[side, step * UNROLL + u] * groups, groups), :]
            for u in range(UNROLL) for side in range(2)]
        for u in range(UNROLL):
            for side in range(2):
                sends[0, side, pl.ds((step * UNROLL + u) * groups, groups), :] = picked[2 * u + side]

    pl.semaphore_wait(barrier, 2 + has_lower.astype(jnp.int32) + has_upper.astype(jnp.int32))
    start(0)

    for load in loads[2:]:
        load.wait()
    first_dir = here * sector
    turn = 2.0 * math.pi / NDIR
    lane_dir = first_dir + lax.broadcasted_iota(jnp.int32, (8, LANES), 1) // 8
    lane_angle = lane_dir.astype(jnp.float32) * turn
    lane_cos, lane_sin = jnp.cos(lane_angle)[:1], jnp.sin(lane_angle)[:1]
    row_dir = first_dir + lax.broadcasted_iota(jnp.int32, (sector, nodes), 0)
    turned = jnp.sin(row_dir.astype(jnp.float32) * turn - refract_angle[...])
    for d in range(sector):
        bearing[d] = turned[d:d + 1]
    gap = jnp.zeros((8 - NEIGH, nodes), jnp.float32)
    edge_cos = edge_speed[...] * jnp.cos(edge_angle[...])
    edge_sin = edge_speed[...] * jnp.sin(edge_angle[...])
    parts = jnp.concatenate([edge_cos, gap, edge_sin, gap], axis=0)
    columns[...] = parts.T

    rows = 32

    @pl.loop(0, nodes // rows)
    def _(step):
        at = pl.multiple_of(step * rows, rows)
        block = columns[pl.ds(at, rows), :]
        places = [pl.ds(at * groups + group, rows, stride=groups) for group in range(groups)]
        base = [scaled[place, :] for place in places]
        found = []
        total = jnp.ones((rows, LANES), jnp.float32)
        for slot in range(NEIGH):
            weight = jnp.maximum(block[:, slot:slot + 1] * lane_cos + block[:, 8 + slot:9 + slot] * lane_sin, 0.0)
            found.append(weight)
            total = total + weight
        inverse = 1.0 / total
        for slot in range(NEIGH):
            weights[pl.ds(slot * nodes + at, rows), :] = found[slot] * inverse
        for group in range(groups):
            f0[places[group], :] = base[group]
            scaled[places[group], :] = base[group] * inverse

    to_table.wait()

    def update(field, start_row, weight_row, extra, row_of):
        total = scaled[pl.ds(start_row, groups), :]
        for slot in range(NEIGH):
            picked = field[pl.ds(row_of(slot), groups), :]
            total = total + weights[pl.ds(weight_row + (slot * nodes + extra), 1), :] * picked
        return total

    def to_next(tile):
        at = pl.ds(pl.multiple_of(tile * LANES, LANES), LANES)
        return pltpu.make_async_remote_copy(
            src_ref=swept.at[sector - 1, :, at], dst_ref=halo.at[0, :, at],
            send_sem=dir_send.at[0, tile], recv_sem=dir_recv.at[0, tile],
            device_id=(dom, next_dir), device_id_type=MESH)

    def to_prev(tile):
        at = pl.ds(pl.multiple_of(tile * LANES, LANES), LANES)
        return pltpu.make_async_remote_copy(
            src_ref=swept.at[0, :, at], dst_ref=halo.at[1, :, at],
            send_sem=dir_send.at[1, tile], recv_sem=dir_recv.at[1, tile],
            device_id=(dom, prev_dir), device_id_type=MESH)

    for sweep in range(SWEEPS):
        field, result = fields[sweep], fields[sweep + 1]
        arrived(sweep)
        if sweep < SWEEPS - 1:
            @pl.loop(0, ghost // UNROLL)
            def _(step):
                totals = []
                for u in range(UNROLL):
                    for side in range(2):
                        node = send_rows[side, step * UNROLL + u]
                        totals.append(update(
                            field, node * groups, node, 0, lambda slot, node=node: shared[slot, node] * groups))
                for u in range(UNROLL):
                    for side in range(2):
                        sends[sweep + 1, side, pl.ds((step * UNROLL + u) * groups, groups), :] = totals[2 * u + side]

            start(sweep + 1)

        def batches(step):
            first = step * BATCH
            first_row = step * (BATCH * groups)
            first_slot = step * 8
            totals = []
            for u in range(BATCH):
                totals.append(update(
                    field, first_row + u * groups, first, u, lambda slot, u=u: table[first_slot + slot, u]))
            for u in range(BATCH):
                result[pl.ds(first_row + u * groups, groups), :] = totals[u]

        if sweep < SWEEPS - 1:
            pl.loop(0, nodes // BATCH)(batches)
        else:
            @pl.loop(0, nodes // LANES)
            def _(tile):
                @pl.loop(0, LANES // BATCH)
                def _(step):
                    batches(tile * (LANES // BATCH) + step)

                at = pl.ds(pl.multiple_of(tile * LANES, LANES), LANES)
                blocks = [
                    result[pl.ds(tile * (LANES * groups) + group, LANES, stride=groups), :].T
                    for group in range(groups)]
                for group in range(groups):
                    swept[:, group * 8:(group + 1) * 8, at] = blocks[group].reshape(sector, 8, LANES)
                to_next(tile).start()
                to_prev(tile).start()

    freq = lax.broadcasted_iota(jnp.int32, (freqs, LANES), 0)

    def finish(d, before, after):
        places = [pl.ds(tile * LANES, LANES) for tile in range(nodes // LANES)]
        found = []
        for at in places:
            own = swept[d, :, at]
            speed = refract_rate[:, at] * bearing[d, :, at]
            refracted = own - (jnp.maximum(speed, 0.0) * (own - before(at)) + jnp.minimum(speed, 0.0) * (after(at) - own))
            lower = jnp.where(freq == 0, 0.0, pltpu.roll(refracted, 1, 0))
            upper = jnp.where(freq == freqs - 1, 0.0, pltpu.roll(refracted, freqs - 1, 0))
            rate = shift_rate[:, at]
            found.append(refracted - (
                jnp.maximum(rate, 0.0) * (refracted - lower) + jnp.minimum(rate, 0.0) * (upper - refracted)))
        for at, value in zip(places, found):
            out[d, :, at] = value

    @pl.loop(1, sector - 1)
    def _(d):
        finish(d, lambda at: swept[d - 1, :, at], lambda at: swept[d + 1, :, at])

    for tile in range(nodes // LANES):
        to_next(tile).wait()
    finish(0, lambda at: halo[0, :, at], lambda at: swept[1, :, at])
    for tile in range(nodes // LANES):
        to_prev(tile).wait()
    finish(sector - 1, lambda at: swept[sector - 2, :, at], lambda at: halo[1, :, at])

    for sweep in range(SWEEPS):
        @pl.when(has_lower)
        def _():
            to_lower(sweep).wait_send()

        @pl.when(has_upper)
        def _():
            to_upper(sweep).wait_send()


def shards(
    action, edge_angle, edge_speed, neighbours, send_rows, refract_rate, refract_angle, shift_rate
):
    sector, freqs, nodes = action.shape
    ghost = send_rows.shape[1]
    groups = freqs // 8
    sizes = (sector, freqs, nodes, ghost, groups, lax.axis_size("dom"), lax.axis_size("dir"))
    field = pltpu.VMEM(((nodes + 2 * ghost) * groups, LANES), jnp.float32)
    local = pltpu.VMEM((nodes * groups, LANES), jnp.float32)
    return pl.pallas_call(
        functools.partial(kernel, sizes),
        out_shape=pltpu.VMEM(action.shape, jnp.float32),
        in_specs=[pl.BlockSpec(memory_space=pltpu.HBM)] * 8,
        out_specs=pl.BlockSpec(memory_space=pltpu.VMEM),
        scratch_shapes=[
            pltpu.VMEM(action.shape, jnp.float32),
            pltpu.VMEM(edge_angle.shape, jnp.float32),
            pltpu.VMEM(edge_speed.shape, jnp.float32),
            pltpu.VMEM(neighbours.shape, jnp.int32),
            pltpu.SMEM(send_rows.shape, jnp.int32),
            pltpu.VMEM(refract_rate.shape, jnp.float32),
            pltpu.VMEM((1, nodes), jnp.float32),
            pltpu.VMEM(shift_rate.shape, jnp.float32),
            pltpu.SMEM(neighbours.shape, jnp.int32),
            pltpu.VMEM((nodes // BATCH * 8, LANES), jnp.int32),
            pltpu.SMEM((nodes // BATCH * 8, LANES), jnp.int32),
            pltpu.SemaphoreType.DMA((9 + groups,)),
            field, field, field, local, local,
            pltpu.VMEM((NEIGH * nodes, LANES), jnp.float32),
            pltpu.VMEM((nodes, 16), jnp.float32),
            pltpu.VMEM((sector, freqs, nodes), jnp.float32),
            pltpu.VMEM((sector, 1, nodes), jnp.float32),
            pltpu.VMEM((SWEEPS, 2, ghost * groups, LANES), jnp.float32),
            pltpu.VMEM((2, freqs, nodes), jnp.float32),
            pltpu.SemaphoreType.DMA((SWEEPS, 2)),
            pltpu.SemaphoreType.DMA((SWEEPS, 2)),
            pltpu.SemaphoreType.DMA((2, nodes // LANES)),
            pltpu.SemaphoreType.DMA((2, nodes // LANES)),
        ],
        compiler_params=pltpu.CompilerParams(
            collective_id=0, has_side_effects=True, vmem_limit_bytes=62 * 1024 * 1024),
    )(action, edge_angle, edge_speed, neighbours, send_rows, refract_rate,
      refract_angle.reshape(1, nodes), shift_rate)


def solution(mesh):
    return jax.shard_map(
        shards,
        mesh=mesh,
        in_specs=(
            P("dir", None, "dom"),
            P(None, "dom"),
            P(None, "dom"),
            P(None, "dom"),
            P(None, "dom"),
            P(None, "dom"),
            P("dom"),
            P(None, "dom"),
        ),
        out_specs=P("dir", None, "dom"),
        check_vma=False,
    )
```
